256 devices in a mesh: ctx: 32 (over y, x, core), head: 8 (over z).
Axes of the slice: x: 4, y: 4, z: 8, core: 2. Of those that a mesh axis runs over, the one named last changes fastest.
Arguments:
- queries: bfloat16 [32768, 4096], P(('ctx', 'head')), may hold values from -81 to 81
- keys: bfloat16 [32768, 1024], P(('ctx', 'head')), may hold values from -4.05 to 4.05
- values: bfloat16 [32768, 1024], P(('ctx', 'head')), may hold values from -6 to 6
- output_gradient: bfloat16 [32768, 4096], P(('ctx', 'head')), may hold values from -6 to 6
- doc_lengths: int32 [64], replicated, may hold values from 1 to 2048, 32768 in all
Outputs:
- attended: bfloat16 [32768, 4096], P(('ctx', 'head'))
- grad_queries: bfloat16 [32768, 4096], P(('ctx', 'head'))
- key_gradient: bfloat16 [32768, 1024], P(('ctx', 'head'))
- value_gradient: bfloat16 [32768, 1024], P(('ctx', 'head'))
The draws below stay inside these ranges and needn't reach their ends.
Inputs may be any that keep to these rules, and one draw needn't show every extreme that they name: `doc_lengths`: their sum is 32768; one document has exactly 2048 tokens.
All inputs are finite; a program needn't handle non-finite values.
Results may differ from the reference program's by a relative error of at most 0.039.
Values may be sent and summed in bfloat16 or wider, within the bound.
A program may use at most 192 MiB of HBM per device.

```python
import math
import jax
import jax.numpy as jnp
import numpy as np
from jax import lax

QUERY_HEADS = 32
KEY_VALUE_HEADS = 8
HEAD_SIZE = 128
PACKED_TOKENS = 32768
LONGEST_DOC = 2048
NDOCS = 64


def shared_keys(key):
    return jnp.clip(jax.random.normal(key, (PACKED_TOKENS, KEY_VALUE_HEADS, HEAD_SIZE), jnp.float32), -4.0, 4.0)


def draw_keys(key, part):
    sampled_input = shared_keys(key)
    return sampled_input.reshape(PACKED_TOKENS, KEY_VALUE_HEADS * HEAD_SIZE).astype(jnp.bfloat16)


def draw_queries(key, part):
    key = jax.random.fold_in(key, 9)
    new_random_key = jnp.clip(jax.random.normal(key, (PACKED_TOKENS, KEY_VALUE_HEADS, QUERY_HEADS // KEY_VALUE_HEADS, HEAD_SIZE), jnp.float32), -4.0, 4.0)
    return new_random_key.reshape(PACKED_TOKENS, QUERY_HEADS * HEAD_SIZE).astype(jnp.bfloat16)


def steps_of(key, shape, split, low, top_value):
    def one(axis_at, shards_of):
        draws = jax.random.uniform(jax.random.fold_in(jax.random.fold_in(key, 6), axis_at), (shards_of,), jnp.float32, low / len(split), top_value / len(split))
        return jnp.repeat(jnp.exp(draws), shape[axis_at] // shards_of).reshape((-1,) + (1,) * (len(shape) - axis_at - 1))

    factor_of = one(*split[0])
    for cut in split[1:]:
        factor_of = factor_of * one(*cut)
    return factor_of


def length_profile(amount, total, most, skew):
    portions = [(1 << 20) // math.isqrt(grade ** skew) + 1 for grade in range(2, amount + 1)]
    spare, counts = total - most - (amount - 1), [1] * (amount - 1)
    while spare > 0:
        free = [i for i in range(amount - 1) if counts[i] < most]
        mass, remaining = sum([portions[i] for i in free]), spare
        for i in free:
            addition = min(most - counts[i], max(1, remaining * portions[i] // mass), spare)
            counts[i] = counts[i] + addition
            spare = spare - addition
    return np.array([most] + counts)


def uneven_parts(stream_key, count, total, reach, skew):
    if count == 2:
        one = jax.random.randint(stream_key, (), max(1, total - reach), min(reach, total - 1) + 1)
        return jnp.stack([one, total - one])
    tallies = jnp.asarray(length_profile(count, total, reach, skew), jnp.int32)
    couples = (count - 1) // 2
    donor, sink = tallies[1:1 + 2 * couples:2], tallies[2:2 + 2 * couples:2]
    margin = jnp.minimum(donor - 1, reach - sink)
    passed = jax.random.randint(jax.random.fold_in(stream_key, 1), (couples,), 0, 1 << 20) % (margin + 1)
    tallies = tallies.at[1:1 + 2 * couples:2].set(donor - passed).at[2:2 + 2 * couples:2].set(sink + passed)
    return tallies[jax.random.permutation(jax.random.fold_in(stream_key, 2), count)]


def centred(rng, shape, deviation, reach, cuts=(), kind=jnp.bfloat16):
    level = steps_of(rng, shape, cuts, -0.22, 0.18) if cuts else 1.0
    drawn = jax.random.normal(rng, shape, jnp.float32) * deviation * level
    return jnp.minimum(jnp.maximum(drawn, -reach), reach).astype(kind)


def setup_inputs(seed: int = 0) -> dict:
    streams_of = jax.random.split(jax.random.key(seed), 6)
    queries = draw_queries(jax.random.fold_in(streams_of[5], 71), 0)
    keys = draw_keys(jax.random.fold_in(streams_of[5], 71), 0)
    values = centred(streams_of[2], (PACKED_TOKENS, KEY_VALUE_HEADS * HEAD_SIZE), 1.0, 6.0, ((0, 256),))
    output_gradient = centred(streams_of[3], (PACKED_TOKENS, QUERY_HEADS * HEAD_SIZE), 1.0, 6.0, ((0, 256),))
    doc_lengths = uneven_parts(streams_of[4], NDOCS, PACKED_TOKENS, LONGEST_DOC, 2).astype(jnp.int32)
    return dict(queries=queries, keys=keys, values=values, output_gradient=output_gradient, doc_lengths=doc_lengths)


def document_ids(doc_lengths, positions):
    doc_ends = jnp.cumsum(doc_lengths).astype(jnp.int32)
    counted = jnp.sum((doc_ends[None, :] <= positions[:, None]).astype(jnp.int32), axis=1)
    return jnp.where(positions < 0, -1, counted).astype(jnp.int32)


def reference(queries, keys, values, output_gradient, doc_lengths):
    query_group_width = QUERY_HEADS // KEY_VALUE_HEADS
    scale_factor = HEAD_SIZE ** -0.5
    tile_rows = min(256, PACKED_TOKENS)
    key_span = LONGEST_DOC + tile_rows
    query_rows_4d = queries.reshape(PACKED_TOKENS, KEY_VALUE_HEADS, query_group_width, HEAD_SIZE)
    output_gradient_4d = output_gradient.reshape(PACKED_TOKENS, KEY_VALUE_HEADS, query_group_width, HEAD_SIZE)
    padding_width = jnp.zeros((LONGEST_DOC, KEY_VALUE_HEADS, HEAD_SIZE), jnp.bfloat16)
    key_rows_3d = jnp.concatenate([padding_width, keys.reshape(PACKED_TOKENS, KEY_VALUE_HEADS, HEAD_SIZE)], axis=0)
    value_rows_3d = jnp.concatenate([padding_width, values.reshape(PACKED_TOKENS, KEY_VALUE_HEADS, HEAD_SIZE)], axis=0)
    padded_pos = jnp.arange(PACKED_TOKENS + LONGEST_DOC, dtype=jnp.int32) - LONGEST_DOC
    padded_doc = document_ids(doc_lengths, padded_pos)

    def block_step(carried, offset):
        key_gradient_total, value_gradient_total = carried
        query_block = lax.dynamic_slice_in_dim(query_rows_4d, offset, tile_rows, 0).astype(jnp.float32)
        grad_block = lax.dynamic_slice_in_dim(output_gradient_4d, offset, tile_rows, 0).astype(jnp.float32)
        key_block = lax.dynamic_slice_in_dim(key_rows_3d, offset, key_span, 0).astype(jnp.float32)
        value_block = lax.dynamic_slice_in_dim(value_rows_3d, offset, key_span, 0).astype(jnp.float32)
        query_doc = lax.dynamic_slice_in_dim(padded_doc, offset + LONGEST_DOC, tile_rows, 0)
        key_doc = lax.dynamic_slice_in_dim(padded_doc, offset, key_span, 0)
        query_pos = offset + jnp.arange(tile_rows, dtype=jnp.int32)
        key_pos = offset - LONGEST_DOC + jnp.arange(key_span, dtype=jnp.int32)
        allowed = (query_doc[:, None] == key_doc[None, :]) & (key_pos[None, :] <= query_pos[:, None])
        scores = jnp.einsum("qhgd,khd->hgqk", query_block, key_block) * scale_factor
        scores = jnp.where(allowed, scores, -jnp.inf)
        row_max = jnp.max(scores, axis=-1, keepdims=True)
        row_total = jnp.sum(jnp.exp(scores - row_max), axis=-1, keepdims=True)
        log_total = row_max + jnp.log(row_total)
        prob = jnp.where(allowed, jnp.exp(scores - log_total), 0.0)
        weights = lax.optimization_barrier(prob.astype(jnp.bfloat16)).astype(jnp.float32)
        attended = jnp.einsum("hgqk,khd->qhgd", weights, value_block).astype(jnp.bfloat16)
        attended_wide = lax.optimization_barrier(attended).astype(jnp.float32)
        row_delta = jnp.einsum("qhgd,qhgd->hgq", grad_block, attended_wide)
        grad_weights = jnp.einsum("qhgd,khd->hgqk", grad_block, value_block)
        grad_scores = lax.optimization_barrier((prob * (grad_weights - row_delta[..., None])).astype(jnp.bfloat16)).astype(jnp.float32)
        grad_query = (scale_factor * jnp.einsum("hgqk,khd->qhgd", grad_scores, key_block)).astype(jnp.bfloat16)
        key_term = jnp.einsum("hgqk,qhgd->khd", grad_scores, query_block)
        value_term = jnp.einsum("hgqk,qhgd->khd", weights, grad_block)
        key_gradient_total = lax.dynamic_update_slice_in_dim(key_gradient_total, lax.dynamic_slice_in_dim(key_gradient_total, offset, key_span, 0) + key_term, offset, 0)
        value_gradient_total = lax.dynamic_update_slice_in_dim(value_gradient_total, lax.dynamic_slice_in_dim(value_gradient_total, offset, key_span, 0) + value_term, offset, 0)
        return (key_gradient_total, value_gradient_total), (attended, grad_query)

    initial_zero_total = jnp.zeros((PACKED_TOKENS + LONGEST_DOC, KEY_VALUE_HEADS, HEAD_SIZE), jnp.float32)
    offsets = jnp.arange(PACKED_TOKENS // tile_rows, dtype=jnp.int32) * tile_rows
    (key_gradient_total, value_gradient_total), (attended, grad_query) = lax.scan(block_step, (initial_zero_total, initial_zero_total), offsets)
    key_gradient = (scale_factor * key_gradient_total[LONGEST_DOC:]).astype(jnp.bfloat16).reshape(PACKED_TOKENS, KEY_VALUE_HEADS * HEAD_SIZE)
    value_gradient = value_gradient_total[LONGEST_DOC:].astype(jnp.bfloat16).reshape(PACKED_TOKENS, KEY_VALUE_HEADS * HEAD_SIZE)
    return attended.reshape(PACKED_TOKENS, QUERY_HEADS * HEAD_SIZE), grad_query.reshape(PACKED_TOKENS, QUERY_HEADS * HEAD_SIZE), key_gradient, value_gradient
```

```python
import math

import jax
import jax.numpy as jnp
from jax import lax
from jax.experimental import pallas as pl
from jax.experimental.pallas import tpu as pltpu
from jax.sharding import PartitionSpec as P

MESH = pl.DeviceIdType.MESH
D = 128
G = 4
B = 128
PEERS = 8
RING = 8
REACH = 2
SLOTS = PEERS + REACH
CHUNKS = 4
TILE = 256
PAD = 128
KEYS = SLOTS * RING * B
SCALE = D ** (-0.5)
LOG2E = math.log2(math.e)
BF16 = jnp.bfloat16
F32 = jnp.float32


def wrap(a, n):
    return lax.rem(a, n)


def place():
    ctx = lax.axis_index("ctx")
    z = lax.axis_index("head")
    group = lax.div(ctx, PEERS)
    return ctx, z, group, ctx - group * PEERS


def enter(devices):
    barrier = pltpu.get_barrier_semaphore()
    for device in devices:
        pl.semaphore_signal(barrier, inc=1, device_id=device, device_id_type=MESH)
    pl.semaphore_wait(barrier, len(devices))


def neighbours(ctx, z, group, me):
    peers = [(group * PEERS + wrap(me + d, PEERS), z) for d in range(1, PEERS)]
    right, left = (ctx, wrap(z + 1, RING)), (ctx, wrap(z + RING - 1, RING))
    groups = lax.axis_size("ctx") // PEERS
    above = (wrap(group + 1, groups) * PEERS + me, z)
    below = (wrap(group + groups - 1, groups) * PEERS + me, z)
    return peers, right, left, above, below


def remote(src, dst, send, recv, device):
    return pltpu.make_async_remote_copy(
        src_ref=src, dst_ref=dst, send_sem=send, recv_sem=recv, device_id=device, device_id_type=MESH
    )


def gather_kernel(
    q_ref, k_ref, v_ref, g_ref, qh_ref, gh_ref, kv_ref,
    kv_send, kv_recv, row_send, row_recv, ring_send, ring_recv, halo_send, halo_recv, own_sem,
):
    ctx, z, group, me = place()
    peers, right, left, above, below = neighbours(ctx, z, group, me)
    enter(peers + [right, left, above, below])

    def lanes(head, width):
        return pl.ds(pl.multiple_of(head * width, width), width)

    own = [
        pltpu.make_async_copy(k_ref.at[:, lanes(me, D)], kv_ref.at[0, REACH + me, z], own_sem.at[0]),
        pltpu.make_async_copy(v_ref.at[:, lanes(me, D)], kv_ref.at[1, REACH + me, z], own_sem.at[1]),
        pltpu.make_async_copy(q_ref.at[:, lanes(me, G * D)], qh_ref.at[me], own_sem.at[2]),
        pltpu.make_async_copy(g_ref.at[:, lanes(me, G * D)], gh_ref.at[me], own_sem.at[3]),
    ]
    kv_copies, row_copies = [], []
    for d in range(1, PEERS):
        head = wrap(me + d, PEERS)
        for part, ref in enumerate((k_ref, v_ref)):
            kv_copies.append(
                remote(
                    ref.at[:, lanes(head, D)], kv_ref.at[part, REACH + me, z],
                    kv_send.at[part, d - 1], kv_recv.at[part, d - 1], peers[d - 1],
                )
            )
        for part, (ref, out) in enumerate(((q_ref, qh_ref), (g_ref, gh_ref))):
            row_copies.append(
                remote(
                    ref.at[:, lanes(head, G * D)], out.at[me],
                    row_send.at[part, d - 1], row_recv.at[part, d - 1], peers[d - 1],
                )
            )
    for copy in own[:2] + kv_copies:
        copy.start()
    for copy in own[:2]:
        copy.wait()
    for copy in kv_copies:
        copy.wait()

    def piece(chunk, offset):
        return kv_ref.at[:, pl.ds(REACH + 2 * chunk, 2), wrap(z + offset + RING, RING)]

    ring = {}
    for way, device in ((0, right), (1, left)):
        for step in range(4):
            for chunk in range(CHUNKS):
                if step == 3 and (chunk < 2) != (way == 0):
                    continue
                block = piece(chunk, -step if way == 0 else step)
                ring[way, step, chunk] = remote(
                    block, block, ring_send.at[way, step, chunk], ring_recv.at[way, step, chunk], device
                )
    halo = []

    def send_halo(offset):
        number = len(halo)
        where = wrap(z + offset + RING, RING)
        copy = remote(
            kv_ref.at[:, pl.ds(PEERS, REACH), where], kv_ref.at[:, pl.ds(0, REACH), where],
            halo_send.at[number], halo_recv.at[number], above,
        )
        copy.start()
        halo.append(copy)

    order = (3, 0, 2, 1)
    for chunk in order:
        for way in (0, 1):
            ring[way, 0, chunk].start()
    send_halo(0)
    for copy in own[2:] + row_copies:
        copy.start()
    for step in range(4):
        for chunk in order:
            for way in (0, 1):
                if (way, step, chunk) not in ring:
                    continue
                ring[way, step, chunk].wait_recv()
                if (way, step + 1, chunk) in ring:
                    ring[way, step + 1, chunk].start()
                if chunk == 3:
                    send_halo(-(step + 1) if way == 0 else step + 1)
    for copy in own[2:] + row_copies:
        copy.wait()
    for copy in ring.values():
        copy.wait_send()
    for copy in halo:
        copy.wait()


def gather(queries, keys, values, gradient):
    anywhere = pl.BlockSpec(memory_space=pl.ANY)
    dma = pltpu.SemaphoreType.DMA
    return pl.pallas_call(
        gather_kernel,
        out_shape=(
            jax.ShapeDtypeStruct((PEERS, B, G * D), BF16),
            jax.ShapeDtypeStruct((PEERS, B, G * D), BF16),
            jax.ShapeDtypeStruct((2, SLOTS, RING, B, D), BF16),
        ),
        in_specs=[anywhere] * 4,
        out_specs=[anywhere] * 3,
        scratch_shapes=[
            dma((2, PEERS - 1)), dma((2, PEERS - 1)), dma((2, PEERS - 1)), dma((2, PEERS - 1)),
            dma((2, 4, CHUNKS)), dma((2, 4, CHUNKS)), dma((RING,)), dma((RING,)), dma((4,)),
        ],
        compiler_params=pltpu.CompilerParams(collective_id=0, has_side_effects=True),
        name="gather",
    )(queries, keys, values, gradient)


def attention_kernel(
    length_ref, q_ref, g_ref, kv_ref, att_ref, dq_ref, dkv_ref,
    kv, dk, dv, score, acc, starts, stage, bounds, load_sem, store_sem,
):
    step = pl.program_id(0)
    _, z, group, _ = place()
    base = (group * PEERS - REACH) * (RING * B)
    first = base + REACH * RING * B + z * B

    def fetch(part, slot):
        rows = RING * B
        return pltpu.make_async_copy(
            kv_ref.at[part, slot], kv.at[part, pl.ds(PAD + slot * rows, rows)], load_sem.at[part, slot]
        )

    @pl.when(step == 0)
    def _():
        for slot in range(SLOTS):
            for part in range(2):
                fetch(part, slot).start()
        kv[:, :PAD, :] = jnp.zeros((2, PAD, D), BF16)
        dk[...] = jnp.zeros_like(dk)
        dv[...] = jnp.zeros_like(dv)
        shape = (PEERS, B)
        positions = (
            first
            + lax.broadcasted_iota(jnp.int32, shape, 0) * (RING * B)
            + lax.broadcasted_iota(jnp.int32, shape, 1)
        )

        def one_doc(number, carried):
            start, vector, low, high = carried
            vector = jnp.where(positions >= start, start, vector)
            low = [jnp.where(first + i * (RING * B) >= start, start, low[i]) for i in range(PEERS)]
            high = [
                jnp.where(first + i * (RING * B) + B - 1 >= start, start, high[i]) for i in range(PEERS)
            ]
            return start + length_ref[number], vector, low, high

        zero = jnp.int32(0)
        _, vector, low, high = lax.fori_loop(
            0, length_ref.shape[0], one_doc,
            (zero, jnp.zeros(shape, jnp.int32), [zero] * PEERS, [zero] * PEERS),
        )
        starts[...] = vector
        for i in range(PEERS):
            bounds[0, i] = low[i]
            bounds[1, i] = high[i]
        for slot in range(SLOTS):
            for part in range(2):
                fetch(part, slot).wait()

    def heads(ref):
        return jnp.concatenate([ref[0, :, h * D : (h + 1) * D] for h in range(G)], axis=0)

    origin = first + step * (RING * B) - base + PAD
    end = origin + B
    low = bounds[0, step] - base + PAD
    high = bounds[1, step] - base + PAD
    tiles = lax.div(end - low + TILE - 1, TILE)
    queries, gradient = heads(q_ref), heads(g_ref)
    start_row = starts[pl.ds(step, 1), :] - base + PAD
    start_row = jnp.concatenate([start_row] * G, axis=1)
    token_row = origin + lax.rem(lax.broadcasted_iota(jnp.int32, (1, G * B), 1), B)

    def rows_of(tile):
        return pl.ds(pl.multiple_of(end - (tile + 1) * TILE, 128), TILE)

    def fold(x, op):
        return op(x.reshape(TILE // 8, 8, G * B), axis=0)

    def first_pass(tile, top):
        s = lax.dot_general(
            kv[0, rows_of(tile), :], queries, (((1,), (1,)), ((), ())), preferred_element_type=F32
        )
        at = end - (tile + 1) * TILE

        def masked(s):
            row = at + lax.broadcasted_iota(jnp.int32, s.shape, 0)
            return jnp.where((row >= start_row) & (row <= token_row), s, -1e30)

        s = lax.cond((tile == 0) | (at < high), masked, lambda s: s, s)
        score[tile] = s
        return jnp.maximum(top, fold(s, jnp.max))

    top = lax.fori_loop(0, tiles, first_pass, jnp.full((8, G * B), -1e30, F32))
    top = jnp.max(top, axis=0, keepdims=True)

    acc[...] = jnp.zeros_like(acc)

    def second_pass(tile, total):
        e = jnp.exp2((score[tile] - top) * (SCALE * LOG2E))
        score[tile] = e
        acc[...] += lax.dot_general(
            kv[1, rows_of(tile), :], e.astype(BF16), (((0,), (0,)), ((), ())), preferred_element_type=F32
        )
        return total + fold(e, jnp.sum)

    total = lax.fori_loop(0, tiles, second_pass, jnp.zeros((8, G * B), F32))
    inverse = 1.0 / jnp.sum(total, axis=0, keepdims=True)
    attended = (acc[...] * inverse).astype(BF16).astype(F32)
    turned = jnp.concatenate([gradient[h * B : (h + 1) * B].astype(F32).T for h in range(G)], axis=1)
    delta = jnp.sum(attended * turned, axis=0, keepdims=True)
    for h in range(G):
        att_ref[0, :, h * D : (h + 1) * D] = attended[:, h * B : (h + 1) * B].T.astype(BF16)

    acc[...] = jnp.zeros_like(acc)

    def third_pass(tile, carried):
        rows = rows_of(tile)
        dp = lax.dot_general(
            kv[1, rows, :], gradient, (((1,), (1,)), ((), ())), preferred_element_type=F32
        )
        p = score[tile] * inverse
        ds = (p * (dp - delta)).astype(BF16)
        dv[rows, :] += jnp.dot(p.astype(BF16), gradient, preferred_element_type=F32)
        dk[rows, :] += jnp.dot(ds, queries, preferred_element_type=F32)
        acc[...] += lax.dot_general(
            kv[0, rows, :], ds, (((0,), (0,)), ((), ())), preferred_element_type=F32
        )
        return carried

    lax.fori_loop(0, tiles, third_pass, 0)
    for h in range(G):
        dq_ref[0, :, h * D : (h + 1) * D] = (SCALE * acc[:, h * B : (h + 1) * B].T).astype(BF16)

    def put(part, slot):
        return pltpu.make_async_copy(stage.at[part, slot], dkv_ref.at[part, slot], store_sem.at[part, slot])

    def finish(slot):
        rows = RING * B
        at = pl.ds(pl.multiple_of(PAD + slot * rows, 128), rows)
        stage[0, slot] = (SCALE * dk[at, :]).astype(BF16)
        stage[1, slot] = dv[at, :].astype(BF16)
        put(0, slot).start()
        put(1, slot).start()

    finish(step)

    @pl.when(step == PEERS - 1)
    def _():
        for slot in range(PEERS, SLOTS):
            finish(slot)
        for slot in range(SLOTS):
            put(0, slot).wait()
            put(1, slot).wait()


def attention(doc_lengths, queries, gradient, kv):
    block = pl.BlockSpec((1, B, G * D), lambda i, *_: (i, 0, 0))
    anywhere = pl.BlockSpec(memory_space=pl.ANY)
    shard = RING * B
    return pl.pallas_call(
        attention_kernel,
        grid_spec=pltpu.PrefetchScalarGridSpec(
            num_scalar_prefetch=1,
            grid=(PEERS,),
            in_specs=[block, block, anywhere],
            out_specs=[block, block, anywhere],
            scratch_shapes=[
                pltpu.VMEM((2, PAD + KEYS, D), BF16),
                pltpu.VMEM((PAD + KEYS, D), F32),
                pltpu.VMEM((PAD + KEYS, D), F32),
                pltpu.VMEM((9, TILE, G * B), F32),
                pltpu.VMEM((D, G * B), F32),
                pltpu.VMEM((PEERS, B), jnp.int32),
                pltpu.VMEM((2, SLOTS, shard, D), BF16),
                pltpu.SMEM((2, PEERS), jnp.int32),
                pltpu.SemaphoreType.DMA((2, SLOTS)),
                pltpu.SemaphoreType.DMA((2, SLOTS)),
            ],
        ),
        out_shape=(
            jax.ShapeDtypeStruct((PEERS, B, G * D), BF16),
            jax.ShapeDtypeStruct((PEERS, B, G * D), BF16),
            jax.ShapeDtypeStruct((2, SLOTS, shard, D), BF16),
        ),
        compiler_params=pltpu.CompilerParams(vmem_limit_bytes=50 * 2**20),
        name="attention",
    )(doc_lengths, queries, gradient, kv.reshape(2, SLOTS, shard, D))


def scatter_kernel(
    att_ref, dq_ref, part_ref, att_out, dq_out, dk_out, dv_out,
    buf, fresh, halo_buf, done,
    row_send, row_recv, ring_send, ring_recv, halo_send, halo_recv, kv_send, kv_recv, own_sem,
):
    ctx, z, group, me = place()
    peers, right, left, above, below = neighbours(ctx, z, group, me)
    enter(peers + [right, left, above, below])

    def lanes(head, width):
        return pl.ds(pl.multiple_of(head * width, width), width)

    halo = {}
    for offset in (4, 3, 5, 2, 6, 1, 7, 0):
        halo[offset] = remote(
            part_ref.at[:, pl.ds(0, REACH), wrap(z + offset, RING)], halo_buf.at[offset],
            halo_send.at[offset], halo_recv.at[offset], below,
        )

    def piece(chunk, offset):
        return part_ref.at[:, pl.ds(REACH + 2 * chunk, 2), wrap(z + offset, RING)]

    def part(chunk, offset):
        value = piece(chunk, offset)[...].astype(F32)
        if chunk == CHUNKS - 1:
            value = value + halo_buf[offset].astype(F32)
        return value

    hops_of = lambda way, chunk: 4 if (chunk < 2) == (way == 0) else 3
    offset_of = lambda way, hops: hops if way == 0 else (RING - hops) % RING
    ring = {}
    for way, device in ((0, right), (1, left)):
        for chunk in range(CHUNKS):
            for hops in range(1, hops_of(way, chunk) + 1):
                if hops < hops_of(way, chunk):
                    source = buf.at[way, hops, chunk]
                elif chunk == CHUNKS - 1:
                    source = fresh.at[way]
                else:
                    source = piece(chunk, offset_of(way, hops))
                ring[way, hops, chunk] = remote(
                    source, buf.at[way, hops - 1, chunk],
                    ring_send.at[way, hops - 1, chunk], ring_recv.at[way, hops - 1, chunk], device,
                )
    own, rows = [], []
    for number, (ref, out) in enumerate(((att_ref, att_out), (dq_ref, dq_out))):
        own.append(pltpu.make_async_copy(ref.at[me], out.at[:, lanes(me, G * D)], own_sem.at[number]))
        for d in range(1, PEERS):
            rows.append(
                remote(
                    ref.at[wrap(me + d, PEERS)], out.at[:, lanes(me, G * D)],
                    row_send.at[number, d - 1], row_recv.at[number, d - 1], peers[d - 1],
                )
            )

    order = (0, 2, 1, 3)
    for turn in range(4):
        for chunk in order:
            for way in (0, 1):
                hops = hops_of(way, chunk) - turn
                if hops < 1:
                    continue
                offset = offset_of(way, hops)
                if chunk == CHUNKS - 1:
                    halo[offset].wait_recv()
                if turn:
                    ring[way, hops + 1, chunk].wait_recv()
                    mine = buf.at[way, hops, chunk]
                    mine[...] = (mine[...].astype(F32) + part(chunk, offset)).astype(BF16)
                elif chunk == CHUNKS - 1:
                    fresh[way] = part(chunk, offset).astype(BF16)
                ring[way, hops, chunk].start()
            if turn == 0 and chunk == order[0]:
                for copy in halo.values():
                    copy.start()
        if turn == 0:
            for copy in own + rows:
                copy.start()
    halo[0].wait_recv()
    last = []
    for chunk in order:
        for way in (0, 1):
            ring[way, 1, chunk].wait_recv()
        value = part(chunk, 0) + buf[0, 0, chunk].astype(F32) + buf[1, 0, chunk].astype(F32)
        done[:, 2 * chunk : 2 * chunk + 2] = value.astype(BF16)
    for number, out in enumerate((dk_out, dv_out)):
        own.append(
            pltpu.make_async_copy(done.at[number, me], out.at[:, lanes(me, D)], own_sem.at[2 + number])
        )
        own[-1].start()
        for d in range(1, PEERS):
            last.append(
                remote(
                    done.at[number, wrap(me + d, PEERS)], out.at[:, lanes(me, D)],
                    kv_send.at[number, d - 1], kv_recv.at[number, d - 1], peers[d - 1],
                )
            )
            last[-1].start()
    for copy in own + rows + last:
        copy.wait()
    for copy in ring.values():
        copy.wait_send()
    for copy in halo.values():
        copy.wait_send()


def scatter(attended, grad_queries, parts):
    anywhere = pl.BlockSpec(memory_space=pl.ANY)
    dma = pltpu.SemaphoreType.DMA
    return pl.pallas_call(
        scatter_kernel,
        out_shape=(
            jax.ShapeDtypeStruct((B, PEERS * G * D), BF16),
            jax.ShapeDtypeStruct((B, PEERS * G * D), BF16),
            jax.ShapeDtypeStruct((B, PEERS * D), BF16),
            jax.ShapeDtypeStruct((B, PEERS * D), BF16),
        ),
        in_specs=[anywhere, anywhere, pl.BlockSpec(memory_space=pltpu.VMEM)],
        out_specs=[anywhere] * 4,
        scratch_shapes=[
            pltpu.VMEM((2, 4, CHUNKS, 2, 2, B, D), BF16),
            pltpu.VMEM((2, 2, 2, B, D), BF16),
            pltpu.VMEM((RING, 2, REACH, B, D), BF16),
            pltpu.VMEM((2, PEERS, B, D), BF16),
            dma((2, PEERS - 1)), dma((2, PEERS - 1)), dma((2, 4, CHUNKS)), dma((2, 4, CHUNKS)),
            dma((RING,)), dma((RING,)), dma((2, PEERS - 1)), dma((2, PEERS - 1)), dma((4,)),
        ],
        compiler_params=pltpu.CompilerParams(
            collective_id=1, has_side_effects=True, vmem_limit_bytes=40 * 2**20
        ),
        name="scatter",
    )(attended, grad_queries, parts)


def shards(queries, keys, values, output_gradient, doc_lengths):
    query_rows, grad_rows, kv = gather(queries, keys, values, output_gradient)
    attended, grad_queries, parts = attention(doc_lengths, query_rows, grad_rows, kv)
    return scatter(attended, grad_queries, parts.reshape(2, SLOTS, RING, B, D))


def solution(mesh):
    rows = P(("ctx", "head"), None)
    return jax.shard_map(
        shards, mesh=mesh, in_specs=(rows, rows, rows, rows, P()), out_specs=(rows,) * 4, check_vma=False
    )
```

```python
import math

import jax
import jax.numpy as jnp
from jax import lax
from jax.experimental import pallas as pl
from jax.experimental.pallas import tpu as pltpu
from jax.sharding import PartitionSpec as P

MESH = pl.DeviceIdType.MESH
D = 128
G = 4
B = 128
PEERS = 8
RING = 8
REACH = 2
SLOTS = PEERS + REACH
CHUNKS = 4
TILE = 256
SIZES = (4, 2, 1)
PAD = 128
KEYS = SLOTS * RING * B
SCALE = D ** (-0.5)
LOG2E = math.log2(math.e)
BF16 = jnp.bfloat16
F32 = jnp.float32


def wrap(a, n):
    return lax.rem(a, n)


def place():
    ctx = lax.axis_index("ctx")
    z = lax.axis_index("head")
    group = lax.div(ctx, PEERS)
    return ctx, z, group, ctx - group * PEERS


def enter(devices):
    barrier = pltpu.get_barrier_semaphore()
    for device in devices:
        pl.semaphore_signal(barrier, inc=1, device_id=device, device_id_type=MESH)
    pl.semaphore_wait(barrier, len(devices))


def neighbours(ctx, z, group, me):
    peers = [(group * PEERS + wrap(me + d, PEERS), z) for d in range(1, PEERS)]
    right, left = (ctx, wrap(z + 1, RING)), (ctx, wrap(z + RING - 1, RING))
    groups = lax.axis_size("ctx") // PEERS
    above = (wrap(group + 1, groups) * PEERS + me, z)
    below = (wrap(group + groups - 1, groups) * PEERS + me, z)
    return peers, right, left, above, below


def remote(src, dst, send, recv, device):
    return pltpu.make_async_remote_copy(
        src_ref=src, dst_ref=dst, send_sem=send, recv_sem=recv, device_id=device, device_id_type=MESH
    )


def gather_kernel(
    q_ref, k_ref, v_ref, g_ref, qh_ref, gh_ref, kv_ref,
    kv_send, kv_recv, row_send, row_recv, ring_send, ring_recv, halo_send, halo_recv, own_sem,
):
    ctx, z, group, me = place()
    peers, right, left, above, below = neighbours(ctx, z, group, me)
    enter(peers + [right, left, above, below])

    def lanes(head, width):
        return pl.ds(pl.multiple_of(head * width, width), width)

    own = [
        pltpu.make_async_copy(k_ref.at[:, lanes(me, D)], kv_ref.at[0, REACH + me, z], own_sem.at[0]),
        pltpu.make_async_copy(v_ref.at[:, lanes(me, D)], kv_ref.at[1, REACH + me, z], own_sem.at[1]),
        pltpu.make_async_copy(q_ref.at[:, lanes(me, G * D)], qh_ref.at[me], own_sem.at[2]),
        pltpu.make_async_copy(g_ref.at[:, lanes(me, G * D)], gh_ref.at[me], own_sem.at[3]),
    ]
    kv_copies, row_copies = [], []
    for d in range(1, PEERS):
        head = wrap(me + d, PEERS)
        for part, ref in enumerate((k_ref, v_ref)):
            kv_copies.append(
                remote(
                    ref.at[:, lanes(head, D)], kv_ref.at[part, REACH + me, z],
                    kv_send.at[part, d - 1], kv_recv.at[part, d - 1], peers[d - 1],
                )
            )
        for part, (ref, out) in enumerate(((q_ref, qh_ref), (g_ref, gh_ref))):
            row_copies.append(
                remote(
                    ref.at[:, lanes(head, G * D)], out.at[me],
                    row_send.at[part, d - 1], row_recv.at[part, d - 1], peers[d - 1],
                )
            )
    for copy in own[:2] + kv_copies:
        copy.start()
    for copy in own[:2]:
        copy.wait()
    for copy in kv_copies:
        copy.wait()

    def piece(chunk, offset):
        return kv_ref.at[:, pl.ds(REACH + 2 * chunk, 2), wrap(z + offset + RING, RING)]

    ring = {}
    for way, device in ((0, right), (1, left)):
        for step in range(4):
            for chunk in range(CHUNKS):
                if step == 3 and (chunk < 2) != (way == 0):
                    continue
                block = piece(chunk, -step if way == 0 else step)
                ring[way, step, chunk] = remote(
                    block, block, ring_send.at[way, step, chunk], ring_recv.at[way, step, chunk], device
                )
    halo = []

    def send_halo(offset):
        number = len(halo)
        where = wrap(z + offset + RING, RING)
        copy = remote(
            kv_ref.at[:, pl.ds(PEERS, REACH), where], kv_ref.at[:, pl.ds(0, REACH), where],
            halo_send.at[number], halo_recv.at[number], above,
        )
        copy.start()
        halo.append(copy)

    order = (3, 0, 2, 1)
    for chunk in order:
        for way in (0, 1):
            ring[way, 0, chunk].start()
    send_halo(0)
    for copy in own[2:] + row_copies:
        copy.start()
    for step in range(4):
        for chunk in order:
            for way in (0, 1):
                if (way, step, chunk) not in ring:
                    continue
                ring[way, step, chunk].wait_recv()
                if (way, step + 1, chunk) in ring:
                    ring[way, step + 1, chunk].start()
                if chunk == 3:
                    send_halo(-(step + 1) if way == 0 else step + 1)
    for copy in own[2:] + row_copies:
        copy.wait()
    for copy in ring.values():
        copy.wait_send()
    for copy in halo:
        copy.wait()


def gather(queries, keys, values, gradient):
    anywhere = pl.BlockSpec(memory_space=pl.ANY)
    dma = pltpu.SemaphoreType.DMA
    return pl.pallas_call(
        gather_kernel,
        out_shape=(
            jax.ShapeDtypeStruct((PEERS, B, G * D), BF16),
            jax.ShapeDtypeStruct((PEERS, B, G * D), BF16),
            jax.ShapeDtypeStruct((2, SLOTS, RING, B, D), BF16),
        ),
        in_specs=[anywhere] * 4,
        out_specs=[anywhere] * 3,
        scratch_shapes=[
            dma((2, PEERS - 1)), dma((2, PEERS - 1)), dma((2, PEERS - 1)), dma((2, PEERS - 1)),
            dma((2, 4, CHUNKS)), dma((2, 4, CHUNKS)), dma((RING,)), dma((RING,)), dma((4,)),
        ],
        compiler_params=pltpu.CompilerParams(collective_id=0, has_side_effects=True),
        name="gather",
    )(queries, keys, values, gradient)


def attention_kernel(
    length_ref, q_ref, g_ref, kv_ref, att_ref, dq_ref, dkv_ref,
    kv, dk, dv, score, acc, starts, stage, bounds, load_sem, store_sem,
):
    step = pl.program_id(0)
    _, z, group, _ = place()
    base = (group * PEERS - REACH) * (RING * B)
    first = base + REACH * RING * B + z * B

    def fetch(part, slot):
        rows = RING * B
        return pltpu.make_async_copy(
            kv_ref.at[part, slot], kv.at[part, pl.ds(PAD + slot * rows, rows)], load_sem.at[part, slot]
        )

    @pl.when(step == 0)
    def _():
        for slot in range(SLOTS):
            for part in range(2):
                fetch(part, slot).start()
        kv[:, :PAD, :] = jnp.zeros((2, PAD, D), BF16)
        dk[...] = jnp.zeros_like(dk)
        dv[...] = jnp.zeros_like(dv)
        shape = (PEERS, B)
        positions = (
            first
            + lax.broadcasted_iota(jnp.int32, shape, 0) * (RING * B)
            + lax.broadcasted_iota(jnp.int32, shape, 1)
        )

        def one_doc(number, carried):
            start, vector, low = carried
            vector = jnp.where(positions >= start, start, vector)
            low = [jnp.where(first + i * (RING * B) >= start, start, low[i]) for i in range(PEERS)]
            return start + length_ref[number], vector, low

        zero = jnp.int32(0)
        _, vector, low = lax.fori_loop(
            0, length_ref.shape[0], one_doc,
            (zero, jnp.zeros(shape, jnp.int32), [zero] * PEERS),
        )
        starts[...] = vector
        for i in range(PEERS):
            bounds[i] = low[i]
        for slot in range(REACH):
            for part in range(2):
                fetch(part, slot).wait()

    for part in range(2):
        fetch(part, REACH + step).wait()

    def heads(ref):
        return jnp.concatenate([ref[0, :, h * D : (h + 1) * D] for h in range(G)], axis=0)

    origin = first + step * (RING * B) - base + PAD
    end = origin + B
    low = bounds[step] - base + PAD
    tiles = lax.div(end - low + TILE - 1, TILE)
    queries, gradient = heads(q_ref), heads(g_ref)
    start_row = starts[pl.ds(step, 1), :] - base + PAD
    start_row = jnp.concatenate([start_row] * G, axis=1)
    token_row = lax.rem(lax.broadcasted_iota(jnp.int32, (1, G * B), 1), B)

    def sweep(body, carried):
        loops = lax.div(tiles, SIZES[0])
        carried = lax.fori_loop(
            0, loops, lambda i, c: body(i * (SIZES[0] * TILE), SIZES[0] * TILE, c), carried
        )
        left, done = tiles - loops * SIZES[0], loops * SIZES[0]
        for size in SIZES[1:]:
            carried = lax.cond(
                left >= size, lambda c: body(done * TILE, size * TILE, c), lambda c: c, carried
            )
            taken = jnp.where(left >= size, size, 0)
            left, done = left - taken, done + taken
        return carried

    def rows_of(ahead, size):
        return pl.ds(pl.multiple_of(end - ahead - size, 128), size)

    def stored(ahead, size):
        return pl.ds(pl.multiple_of(ahead, TILE), size)

    def fold(x, op):
        return op(x.reshape(x.shape[0] // 8, 8, G * B), axis=0)

    def first_pass(ahead, size, top):
        s = lax.dot_general(
            kv[0, rows_of(ahead, size), :], queries, (((1,), (1,)), ((), ())), preferred_element_type=F32
        )
        row = lax.broadcasted_iota(jnp.int32, s.shape, 0)
        s = jnp.where(row >= start_row - (end - ahead - size), s, -1e30)
        late = s[size - B :]
        row = lax.broadcasted_iota(jnp.int32, late.shape, 0)
        late = jnp.where(row <= token_row + ahead, late, -1e30)
        s = jnp.concatenate([s[: size - B], late], axis=0)
        score[stored(ahead, size), :] = s
        return jnp.maximum(top, fold(s, jnp.max))

    top = sweep(first_pass, jnp.full((8, G * B), -1e30, F32))
    top = jnp.max(top, axis=0, keepdims=True)

    acc[...] = jnp.zeros_like(acc)

    def second_pass(ahead, size, total):
        e = jnp.exp2((score[stored(ahead, size), :] - top) * (SCALE * LOG2E))
        score[stored(ahead, size), :] = e
        acc[...] += lax.dot_general(
            kv[1, rows_of(ahead, size), :], e.astype(BF16), (((0,), (0,)), ((), ())),
            preferred_element_type=F32,
        )
        return total + fold(e, jnp.sum)

    total = sweep(second_pass, jnp.zeros((8, G * B), F32))
    inverse = 1.0 / jnp.sum(total, axis=0, keepdims=True)
    attended = (acc[...] * inverse).astype(BF16).astype(F32)
    turned = jnp.concatenate([gradient[h * B : (h + 1) * B].astype(F32).T for h in range(G)], axis=1)
    delta = jnp.sum(attended * turned, axis=0, keepdims=True)
    for h in range(G):
        att_ref[0, :, h * D : (h + 1) * D] = attended[:, h * B : (h + 1) * B].T.astype(BF16)

    acc[...] = jnp.zeros_like(acc)

    def third_pass(ahead, size, carried):
        rows = rows_of(ahead, size)
        dp = lax.dot_general(
            kv[1, rows, :], gradient, (((1,), (1,)), ((), ())), preferred_element_type=F32
        )
        p = score[stored(ahead, size), :] * inverse
        ds = (p * (dp - delta)).astype(BF16)
        dv[rows, :] += jnp.dot(p.astype(BF16), gradient, preferred_element_type=F32)
        dk[rows, :] += jnp.dot(ds, queries, preferred_element_type=F32)
        acc[...] += lax.dot_general(
            kv[0, rows, :], ds, (((0,), (0,)), ((), ())), preferred_element_type=F32
        )
        return carried

    sweep(third_pass, 0)
    for h in range(G):
        dq_ref[0, :, h * D : (h + 1) * D] = (SCALE * acc[:, h * B : (h + 1) * B].T).astype(BF16)

    def put(part, slot):
        return pltpu.make_async_copy(stage.at[part, slot], dkv_ref.at[part, slot], store_sem.at[part, slot])

    def finish(slot):
        rows = RING * B
        at = pl.ds(pl.multiple_of(PAD + slot * rows, 128), rows)
        stage[0, slot] = (SCALE * dk[at, :]).astype(BF16)
        stage[1, slot] = dv[at, :].astype(BF16)
        put(0, slot).start()
        put(1, slot).start()

    finish(step)

    @pl.when(step == PEERS - 1)
    def _():
        for slot in range(PEERS, SLOTS):
            finish(slot)
        for slot in range(SLOTS):
            put(0, slot).wait()
            put(1, slot).wait()


def attention(doc_lengths, queries, gradient, kv):
    block = pl.BlockSpec((1, B, G * D), lambda i, *_: (i, 0, 0))
    anywhere = pl.BlockSpec(memory_space=pl.ANY)
    shard = RING * B
    return pl.pallas_call(
        attention_kernel,
        grid_spec=pltpu.PrefetchScalarGridSpec(
            num_scalar_prefetch=1,
            grid=(PEERS,),
            in_specs=[block, block, anywhere],
            out_specs=[block, block, anywhere],
            scratch_shapes=[
                pltpu.VMEM((2, PAD + KEYS, D), BF16),
                pltpu.VMEM((PAD + KEYS, D), F32),
                pltpu.VMEM((PAD + KEYS, D), F32),
                pltpu.VMEM((9 * TILE, G * B), F32),
                pltpu.VMEM((D, G * B), F32),
                pltpu.VMEM((PEERS, B), jnp.int32),
                pltpu.VMEM((2, SLOTS, shard, D), BF16),
                pltpu.SMEM((PEERS,), jnp.int32),
                pltpu.SemaphoreType.DMA((2, SLOTS)),
                pltpu.SemaphoreType.DMA((2, SLOTS)),
            ],
        ),
        out_shape=(
            jax.ShapeDtypeStruct((PEERS, B, G * D), BF16),
            jax.ShapeDtypeStruct((PEERS, B, G * D), BF16),
            jax.ShapeDtypeStruct((2, SLOTS, shard, D), BF16),
        ),
        compiler_params=pltpu.CompilerParams(vmem_limit_bytes=50 * 2**20),
        name="attention",
    )(doc_lengths, queries, gradient, kv.reshape(2, SLOTS, shard, D))


def scatter_kernel(
    att_ref, dq_ref, part_ref, att_out, dq_out, dk_out, dv_out,
    buf, fresh, halo_buf, done,
    row_send, row_recv, ring_send, ring_recv, halo_send, halo_recv, kv_send, kv_recv, own_sem,
):
    ctx, z, group, me = place()
    peers, right, left, above, below = neighbours(ctx, z, group, me)
    enter(peers + [right, left, above, below])

    def lanes(head, width):
        return pl.ds(pl.multiple_of(head * width, width), width)

    halo = {}
    for offset in (4, 3, 5, 2, 6, 1, 7, 0):
        halo[offset] = remote(
            part_ref.at[:, pl.ds(0, REACH), wrap(z + offset, RING)], halo_buf.at[offset],
            halo_send.at[offset], halo_recv.at[offset], below,
        )

    def piece(chunk, offset):
        return part_ref.at[:, pl.ds(REACH + 2 * chunk, 2), wrap(z + offset, RING)]

    def part(chunk, offset):
        value = piece(chunk, offset)[...].astype(F32)
        if chunk == CHUNKS - 1:
            value = value + halo_buf[offset].astype(F32)
        return value

    hops_of = lambda way, chunk: 4 if (chunk < 2) == (way == 0) else 3
    offset_of = lambda way, hops: hops if way == 0 else (RING - hops) % RING
    ring = {}
    for way, device in ((0, right), (1, left)):
        for chunk in range(CHUNKS):
            for hops in range(1, hops_of(way, chunk) + 1):
                if hops < hops_of(way, chunk):
                    source = buf.at[way, hops, chunk]
                elif chunk == CHUNKS - 1:
                    source = fresh.at[way]
                else:
                    source = piece(chunk, offset_of(way, hops))
                ring[way, hops, chunk] = remote(
                    source, buf.at[way, hops - 1, chunk],
                    ring_send.at[way, hops - 1, chunk], ring_recv.at[way, hops - 1, chunk], device,
                )
    own, rows = [], []
    for number, (ref, out) in enumerate(((att_ref, att_out), (dq_ref, dq_out))):
        own.append(pltpu.make_async_copy(ref.at[me], out.at[:, lanes(me, G * D)], own_sem.at[number]))
        for d in range(1, PEERS):
            rows.append(
                remote(
                    ref.at[wrap(me + d, PEERS)], out.at[:, lanes(me, G * D)],
                    row_send.at[number, d - 1], row_recv.at[number, d - 1], peers[d - 1],
                )
            )

    order = (0, 2, 1, 3)
    for turn in range(4):
        for chunk in order:
            for way in (0, 1):
                hops = hops_of(way, chunk) - turn
                if hops < 1:
                    continue
                offset = offset_of(way, hops)
                if chunk == CHUNKS - 1:
                    halo[offset].wait_recv()
                if turn:
                    ring[way, hops + 1, chunk].wait_recv()
                    mine = buf.at[way, hops, chunk]
                    mine[...] = (mine[...].astype(F32) + part(chunk, offset)).astype(BF16)
                elif chunk == CHUNKS - 1:
                    fresh[way] = part(chunk, offset).astype(BF16)
                ring[way, hops, chunk].start()
            if turn == 0 and chunk == order[0]:
                for copy in halo.values():
                    copy.start()
        if turn == 0:
            for copy in own + rows:
                copy.start()
    halo[0].wait_recv()
    last = []
    for chunk in order:
        for way in (0, 1):
            ring[way, 1, chunk].wait_recv()
        value = part(chunk, 0) + buf[0, 0, chunk].astype(F32) + buf[1, 0, chunk].astype(F32)
        done[:, 2 * chunk : 2 * chunk + 2] = value.astype(BF16)
    for number, out in enumerate((dk_out, dv_out)):
        own.append(
            pltpu.make_async_copy(done.at[number, me], out.at[:, lanes(me, D)], own_sem.at[2 + number])
        )
        own[-1].start()
        for d in range(1, PEERS):
            last.append(
                remote(
                    done.at[number, wrap(me + d, PEERS)], out.at[:, lanes(me, D)],
                    kv_send.at[number, d - 1], kv_recv.at[number, d - 1], peers[d - 1],
                )
            )
            last[-1].start()
    for copy in own + rows + last:
        copy.wait()
    for copy in ring.values():
        copy.wait_send()
    for copy in halo.values():
        copy.wait_send()


def scatter(attended, grad_queries, parts):
    anywhere = pl.BlockSpec(memory_space=pl.ANY)
    dma = pltpu.SemaphoreType.DMA
    return pl.pallas_call(
        scatter_kernel,
        out_shape=(
            jax.ShapeDtypeStruct((B, PEERS * G * D), BF16),
            jax.ShapeDtypeStruct((B, PEERS * G * D), BF16),
            jax.ShapeDtypeStruct((B, PEERS * D), BF16),
            jax.ShapeDtypeStruct((B, PEERS * D), BF16),
        ),
        in_specs=[anywhere, anywhere, pl.BlockSpec(memory_space=pltpu.VMEM)],
        out_specs=[anywhere] * 4,
        scratch_shapes=[
            pltpu.VMEM((2, 4, CHUNKS, 2, 2, B, D), BF16),
            pltpu.VMEM((2, 2, 2, B, D), BF16),
            pltpu.VMEM((RING, 2, REACH, B, D), BF16),
            pltpu.VMEM((2, PEERS, B, D), BF16),
            dma((2, PEERS - 1)), dma((2, PEERS - 1)), dma((2, 4, CHUNKS)), dma((2, 4, CHUNKS)),
            dma((RING,)), dma((RING,)), dma((2, PEERS - 1)), dma((2, PEERS - 1)), dma((4,)),
        ],
        compiler_params=pltpu.CompilerParams(
            collective_id=1, has_side_effects=True, vmem_limit_bytes=40 * 2**20
        ),
        name="scatter",
    )(attended, grad_queries, parts)


def shards(queries, keys, values, output_gradient, doc_lengths):
    query_rows, grad_rows, kv = gather(queries, keys, values, output_gradient)
    attended, grad_queries, parts = attention(doc_lengths, query_rows, grad_rows, kv)
    return scatter(attended, grad_queries, parts.reshape(2, SLOTS, RING, B, D))


def solution(mesh):
    rows = P(("ctx", "head"), None)
    return jax.shard_map(
        shards, mesh=mesh, in_specs=(rows, rows, rows, rows, P()), out_specs=(rows,) * 4, check_vma=False
    )
```

```python
import math

import jax
import jax.numpy as jnp
from jax import lax
from jax.experimental import pallas as pl
from jax.experimental.pallas import tpu as pltpu
from jax.sharding import PartitionSpec as P

MESH = pl.DeviceIdType.MESH
D = 128
G = 4
B = 128
PEERS = 8
RING = 8
REACH = 2
SLOTS = PEERS + REACH
CHUNKS = 4
SHARD = RING * B
ROWS = G * B
HOPS = 4
UNSEEN = -1e30
SCALE = D ** (-0.5)
LOG2E = math.log2(math.e)
BF16 = jnp.bfloat16
F32 = jnp.float32


def wrap(a, n):
    return lax.rem(a, n)


def place():
    ctx = lax.axis_index("ctx")
    z = lax.axis_index("head")
    group = lax.div(ctx, PEERS)
    return ctx, z, group, ctx - group * PEERS


def enter(devices):
    barrier = pltpu.get_barrier_semaphore()
    for device in devices:
        pl.semaphore_signal(barrier, inc=1, device_id=device, device_id_type=MESH)
    pl.semaphore_wait(barrier, len(devices))


def neighbours(ctx, z, group, me):
    peers = [(group * PEERS + wrap(me + d, PEERS), z) for d in range(1, PEERS)]
    right, left = (ctx, wrap(z + 1, RING)), (ctx, wrap(z + RING - 1, RING))
    groups = lax.axis_size("ctx") // PEERS
    above = (wrap(group + 1, groups) * PEERS + me, z)
    below = (wrap(group + groups - 1, groups) * PEERS + me, z)
    return peers, right, left, above, below


def remote(src, dst, send, recv, device):
    return pltpu.make_async_remote_copy(
        src_ref=src, dst_ref=dst, send_sem=send, recv_sem=recv, device_id=device, device_id_type=MESH
    )


def kernel(
    length_ref, q_ref, k_ref, v_ref, g_ref, att_out, dq_out, dk_out, dv_out,
    kv, qs, gs, acc, top, total, shift, delta, starts, atts, dqs, sums, mine, buf, halo_buf,
    kv_send, kv_recv, row_send, row_recv, ring_send, ring_recv, halo_send, halo_recv,
    out_send, out_recv, back_send, back_recv, gone_send, gone_recv, last_send, last_recv, own_sem,
):
    ctx, z, group, me = place()
    peers, right, left, above, below = neighbours(ctx, z, group, me)
    base = (group * PEERS - REACH) * SHARD
    enter(peers + [right, left, above, below])

    def lanes(head, width):
        if isinstance(head, int):
            return pl.ds(head * width, width)
        return pl.ds(pl.multiple_of(head * width, width), width)

    def at(offset):
        return wrap(z + offset, RING)

    def exchange(ref, width, target, send, recv, own):
        copies = [pltpu.make_async_copy(ref.at[:, lanes(me, width)], target, own)]
        for d in range(1, PEERS):
            head = wrap(me + d, PEERS)
            copies.append(
                remote(ref.at[:, lanes(head, width)], target, send.at[d - 1], recv.at[d - 1], peers[d - 1])
            )
        return copies

    key_copies = [
        copy
        for part, ref in enumerate((k_ref, v_ref))
        for copy in exchange(
            ref, D, kv.at[part, REACH + me, z], kv_send.at[part], kv_recv.at[part], own_sem.at[part]
        )
    ]
    query_copies = exchange(q_ref, G * D, qs.at[me], row_send.at[0], row_recv.at[0], own_sem.at[2])
    grad_copies = exchange(g_ref, G * D, gs.at[me], row_send.at[1], row_recv.at[1], own_sem.at[3])
    for copy in key_copies:
        copy.start()

    positions = (
        base + REACH * SHARD + z * B
        + lax.broadcasted_iota(jnp.int32, (PEERS, B), 0) * SHARD
        + lax.broadcasted_iota(jnp.int32, (PEERS, B), 1)
    )

    def one_doc(number, carried):
        start, vector = carried
        return start + length_ref[number], jnp.where(positions >= start, start, vector)

    _, vector = lax.fori_loop(
        0, length_ref.shape[0], one_doc, (jnp.int32(0), jnp.zeros((PEERS, B), jnp.int32))
    )
    starts[...] = jnp.concatenate([vector - base] * G, axis=1)
    token = lax.rem(lax.broadcasted_iota(jnp.int32, (1, ROWS), 1), B)

    def ring(way, step, chunk):
        offset = step if way else (RING - step) % RING
        block = kv.at[:, pl.ds(REACH + 2 * chunk, 2), at(offset)]
        return remote(
            block, block, ring_send.at[way, step, chunk], ring_recv.at[way, step, chunk], left if way else right
        )

    def halo(offset):
        return remote(
            kv.at[:, pl.ds(PEERS, REACH), at(offset)], kv.at[:, pl.ds(0, REACH), at(offset)],
            halo_send.at[offset], halo_recv.at[offset], above,
        )

    def arrive(step, turn):
        chunk = CHUNKS - 1 - turn
        for way in (0, 1):
            far = (turn < 2) if way else (turn >= 2)
            if step < HOPS:
                ring(way, step - 1, chunk).wait_recv()
            else:
                pl.when(far)(lambda: ring(way, step - 1, chunk).wait_recv())
            if step < HOPS - 1:
                ring(way, step, chunk).start()
            elif step == HOPS - 1:
                pl.when(far)(lambda: ring(way, step, chunk).start())

        @pl.when(turn == 0)
        def _():
            halo(step).start()
            if step < HOPS:
                halo(RING - step).start()

    def rows(ref, i):
        return jnp.concatenate([ref[i, :, h * D : (h + 1) * D] for h in range(G)], axis=0)

    def keys_of(i, offset):
        if offset == 0:
            return i, 3
        return i + lax.div(z + offset, RING), 2

    def scores(i, offset, queries):
        slot, count = keys_of(i, offset)
        where = at(offset)
        keys = kv[0, pl.ds(slot, count), where].reshape(count * B, D)
        s = lax.dot_general(keys, queries, (((1,), (1,)), ((), ())), preferred_element_type=F32)
        limit = starts[pl.ds(i, 1), :] - (slot * SHARD + where * B)
        row = lax.broadcasted_iota(jnp.int32, (B, ROWS), 0)
        parts = []
        for n in range(count):
            seen = row >= limit - n * SHARD
            if offset == 0 and n == count - 1:
                seen = seen & (row <= token)
            parts.append(jnp.where(seen, s[n * B : (n + 1) * B], UNSEEN))
        return keys, jnp.concatenate(parts, axis=0)

    def values_of(i, offset):
        slot, count = keys_of(i, offset)
        return kv[1, pl.ds(slot, count), at(offset)].reshape(count * B, D)

    def fold(x, op):
        return op(x.reshape(x.shape[0] // 8, 8, ROWS), axis=0)

    def turned_dot(a, b):
        return lax.dot_general(a, b, (((0,), (0,)), ((), ())), preferred_element_type=F32)

    def forward(pair, offset):
        blocks = (2 * pair, 2 * pair + 1)
        found = [scores(i, offset, rows(qs, i))[1] for i in blocks]
        high = [jnp.max(fold(s, jnp.max), axis=0, keepdims=True) for s in found]
        before = [None if offset == 0 else top[pl.ds(i, 1), :] for i in blocks]
        if offset:
            high = [jnp.maximum(a, b) for a, b in zip(high, before)]
        e = [jnp.exp2((s - h) * (SCALE * LOG2E)) for s, h in zip(found, high)]
        out = [turned_dot(values_of(i, offset), x.astype(BF16)) for i, x in zip(blocks, e)]
        count = [fold(x, jnp.sum) for x in e]
        if offset:
            less = [jnp.exp2((b - h) * (SCALE * LOG2E)) for b, h in zip(before, high)]
            out = [acc[i] * f + o for i, f, o in zip(blocks, less, out)]
            count = [total[i] * f + c for i, f, c in zip(blocks, less, count)]
        for i, h, o, c in zip(blocks, high, out, count):
            top[pl.ds(i, 1), :] = h
            acc[i] = o
            total[i] = c

    def four(step, offsets):
        def turn(k, carried):
            if step is not None:
                arrive(step, k)

            @pl.when(k == CHUNKS - 1)
            def _():
                for offset in offsets:
                    halo(offset).wait_recv()

            pair = lax.rem(k + 1, PEERS // 2)
            for offset in offsets:
                forward(pair, offset)
            return carried

        lax.fori_loop(0, CHUNKS, turn, 0)

    for copy in key_copies:
        copy.wait()
    for chunk in reversed(range(CHUNKS)):
        for way in (0, 1):
            ring(way, 0, chunk).start()
    halo(0).start()
    for copy in query_copies:
        copy.start()
    for k in range(CHUNKS):
        arrive(1, k)
    for copy in query_copies:
        copy.wait()
    for copy in grad_copies:
        copy.start()
    four(2, (0, 7, 1))
    four(3, (6, 2))
    four(4, (5, 3))
    four(None, (4,))
    for copy in grad_copies:
        copy.wait()

    def close(i, carried):
        count = jnp.sum(total[i], axis=0, keepdims=True)
        attended = (acc[i] * (1.0 / count)).astype(BF16).astype(F32)
        shift[pl.ds(i, 1), :] = top[pl.ds(i, 1), :] * (SCALE * LOG2E) + jnp.log(count) * LOG2E
        turned = jnp.concatenate([gs[i, :, h * D : (h + 1) * D].astype(F32).T for h in range(G)], axis=1)
        delta[pl.ds(i, 1), :] = jnp.sum(attended * turned, axis=0, keepdims=True)
        for h in range(G):
            atts[i, :, h * D : (h + 1) * D] = attended[:, h * B : (h + 1) * B].T.astype(BF16)
        acc[i] = jnp.zeros((D, ROWS), F32)
        return carried

    lax.fori_loop(0, PEERS, close, 0)

    def give(ref, out, width, send, recv, own):
        copies = [pltpu.make_async_copy(ref.at[me], out.at[:, lanes(me, width)], own)]
        for d in range(1, PEERS):
            copies.append(
                remote(
                    ref.at[wrap(me + d, PEERS)], out.at[:, lanes(me, width)],
                    send.at[d - 1], recv.at[d - 1], peers[d - 1],
                )
            )
        for copy in copies:
            copy.start()
        return copies

    given = give(atts, att_out, G * D, out_send.at[0], out_recv.at[0], own_sem.at[4])

    def backward(pair, offset):
        blocks = (2 * pair, 2 * pair + 1)
        slot, count = keys_of(blocks[0], offset)
        queries, grads = [rows(qs, i) for i in blocks], [rows(gs, i) for i in blocks]
        found = [scores(i, offset, q) for i, q in zip(blocks, queries)]
        dp = [
            lax.dot_general(
                values_of(i, offset), g, (((1,), (1,)), ((), ())), preferred_element_type=F32
            )
            for i, g in zip(blocks, grads)
        ]
        p = [
            jnp.exp2(s * (SCALE * LOG2E) - shift[pl.ds(i, 1), :]) for i, (_, s) in zip(blocks, found)
        ]
        ds = [(a * (b - delta[pl.ds(i, 1), :])).astype(BF16) for i, a, b in zip(blocks, p, dp)]
        dk = [jnp.dot(d, q, preferred_element_type=F32) for d, q in zip(ds, queries)]
        dv = [jnp.dot(a.astype(BF16), g, preferred_element_type=F32) for a, g in zip(p, grads)]
        dq = [turned_dot(keys, d) for (keys, _), d in zip(found, ds)]
        for part, (a, b) in enumerate((dk, dv)):
            middle = a[B:] + b[: (count - 1) * B]
            value = jnp.concatenate([a[:B], middle, b[(count - 1) * B :]], axis=0)
            sums[part, pl.ds(slot, count + 1)] += value.reshape(count + 1, B, D)
        for i, d in zip(blocks, dq):
            acc[i] += d

    def all_backward(offset):
        sums[...] = jnp.zeros_like(sums)

        def one(pair, carried):
            backward(pair, offset)
            return carried

        lax.fori_loop(0, PEERS // 2, one, 0)
        for part, scale in enumerate((SCALE, 1.0)):
            mine[offset, part] = (sums[part] * scale).astype(BF16)
        home(offset).start()

    def home(offset):
        return remote(
            mine.at[offset, :, pl.ds(0, REACH)], halo_buf.at[offset],
            back_send.at[offset], back_recv.at[offset], below,
        )

    def piece(chunk, offset):
        return mine.at[offset, :, pl.ds(REACH + 2 * chunk, 2)]

    def add(target, *others):
        target[...] = sum((ref[...].astype(F32) for ref in others), target[...].astype(F32)).astype(BF16)

    def add_halo(offset):
        home(offset).wait_recv()
        add(piece(CHUNKS - 1, offset), halo_buf.at[offset])

    def most(way, chunk):
        return HOPS if (chunk < 2) == (way == 0) else HOPS - 1

    def message(way, hops, chunk):
        first = hops == most(way, chunk)
        source = piece(chunk, (RING - hops) if way else hops) if first else buf.at[way, hops, chunk]
        return remote(
            source, buf.at[way, hops - 1, chunk],
            gone_send.at[way, hops - 1, chunk], gone_recv.at[way, hops - 1, chunk], left if way else right,
        )

    def post(way, hops, *chunks):
        for chunk in chunks:
            if hops < most(way, chunk):
                message(way, hops + 1, chunk).wait_recv()
                add(buf.at[way, hops, chunk], piece(chunk, (RING - hops) if way else hops))
            message(way, hops, chunk).start()

    all_backward(4)
    post(0, 4, 0, 1)
    post(1, 4, 2)
    all_backward(3)
    post(0, 3, 2)
    add_halo(4)
    post(1, 4, 3)
    all_backward(5)
    add_halo(3)
    post(1, 3, 0, 1)
    post(0, 3, 3, 0, 1)
    post(1, 3, 2)
    all_backward(2)
    add_halo(5)
    post(1, 3, 3)
    post(0, 2, 2)
    all_backward(6)
    add_halo(2)
    post(0, 2, 3)
    all_backward(1)
    add_halo(6)
    post(0, 2, 0, 1)
    post(1, 2, 0, 1, 2)
    all_backward(7)
    add_halo(1)
    post(1, 2, 3)
    post(0, 1, 2)
    all_backward(0)

    def close_query(i, carried):
        for h in range(G):
            dqs[i, :, h * D : (h + 1) * D] = (SCALE * acc[i, :, h * B : (h + 1) * B].T).astype(BF16)
        return carried

    lax.fori_loop(0, PEERS, close_query, 0)
    given += give(dqs, dq_out, G * D, out_send.at[1], out_recv.at[1], own_sem.at[5])
    add_halo(7)
    add_halo(0)
    post(0, 1, 3)
    post(1, 1, 0)
    post(0, 1, 0)
    post(1, 1, 1)
    post(0, 1, 1)
    post(1, 1, 2, 3)

    def last(number, j):
        out = dv_out if number else dk_out
        return remote(
            mine.at[0, number, REACH + j], out.at[:, lanes(me, D)],
            last_send.at[number, j], last_recv.at[number, me], (group * PEERS + j, z),
        )

    for chunk in (0, 2, 1, 3):
        for way in (0, 1):
            message(way, 1, chunk).wait_recv()
        add(piece(chunk, 0), buf.at[0, 0, chunk], buf.at[1, 0, chunk])
        for j in (2 * chunk, 2 * chunk + 1):

            @pl.when(j != me)
            def _():
                last(0, j).start()
                last(1, j).start()

    for number, out in enumerate((dk_out, dv_out)):
        given.append(
            pltpu.make_async_copy(
                mine.at[0, number, REACH + me], out.at[:, lanes(me, D)], own_sem.at[6 + number]
            )
        )
        given[-1].start()
    for copy in given:
        copy.wait()
    for j in range(PEERS):

        @pl.when(j != me)
        def _():
            for number, out in enumerate((dk_out, dv_out)):
                remote(
                    mine.at[0, number, REACH + j], out.at[:, lanes(j, D)],
                    last_send.at[number, j], last_recv.at[number, j], (group * PEERS + j, z),
                ).wait()

    for offset in range(RING):
        halo(offset).wait_send()
        home(offset).wait_send()
    for way in (0, 1):
        for chunk in range(CHUNKS):
            for step in range(most(way, chunk)):
                ring(way, step, chunk).wait_send()
                message(way, step + 1, chunk).wait_send()


def shards(queries, keys, values, output_gradient, doc_lengths):
    anywhere = pl.BlockSpec(memory_space=pltpu.HBM)
    dma = pltpu.SemaphoreType.DMA
    block, message = (B, D), (2, 2, B, D)
    peers, hops = (2, PEERS - 1), (2, HOPS, CHUNKS)
    return pl.pallas_call(
        kernel,
        out_shape=[jax.ShapeDtypeStruct(a.shape, BF16) for a in (queries, queries, keys, values)],
        in_specs=[pl.BlockSpec(memory_space=pltpu.SMEM)] + [anywhere] * 4,
        out_specs=[anywhere] * 4,
        scratch_shapes=[
            pltpu.VMEM((2, SLOTS, RING) + block, BF16),
            pltpu.VMEM((PEERS, B, G * D), BF16),
            pltpu.VMEM((PEERS, B, G * D), BF16),
            pltpu.VMEM((PEERS, D, ROWS), F32),
            pltpu.VMEM((PEERS, ROWS), F32),
            pltpu.VMEM((PEERS, 8, ROWS), F32),
            pltpu.VMEM((PEERS, ROWS), F32),
            pltpu.VMEM((PEERS, ROWS), F32),
            pltpu.VMEM((PEERS, ROWS), jnp.int32),
            pltpu.VMEM((PEERS, B, G * D), BF16),
            pltpu.VMEM((PEERS, B, G * D), BF16),
            pltpu.VMEM((2, SLOTS) + block, F32),
            pltpu.VMEM((RING, 2, SLOTS) + block, BF16),
            pltpu.VMEM((2, HOPS, CHUNKS) + message, BF16),
            pltpu.VMEM((RING,) + message, BF16),
            dma(peers), dma(peers), dma(peers), dma(peers), dma(hops), dma(hops), dma((RING,)), dma((RING,)),
            dma(peers), dma(peers), dma((RING,)), dma((RING,)), dma(hops), dma(hops), dma((2, PEERS)), dma((2, PEERS)),
            dma((8,)),
        ],
        compiler_params=pltpu.CompilerParams(
            collective_id=0, has_side_effects=True, vmem_limit_bytes=50 * 2**20
        ),
        name="attention",
    )(doc_lengths, queries, keys, values, output_gradient)


def solution(mesh):
    rows = P(("ctx", "head"), None)
    return jax.shard_map(
        shards, mesh=mesh, in_specs=(rows, rows, rows, rows, P()), out_specs=(rows,) * 4, check_vma=False
    )
```

```python
import math

import jax
import jax.numpy as jnp
from jax import lax
from jax.experimental import pallas as pl
from jax.experimental.pallas import tpu as pltpu
from jax.sharding import PartitionSpec as P

MESH = pl.DeviceIdType.MESH
D = 128
G = 4
B = 128
PEERS = 8
RING = 8
REACH = 2
SLOTS = PEERS + REACH
CHUNKS = 4
SHARD = RING * B
ROWS = G * B
HOPS = 4
UNSEEN = -1e30
SCALE = D ** (-0.5)
LOG2E = math.log2(math.e)
BF16 = jnp.bfloat16
F32 = jnp.float32


def wrap(a, n):
    return lax.rem(a, n)


def place():
    ctx = lax.axis_index("ctx")
    z = lax.axis_index("head")
    group = lax.div(ctx, PEERS)
    return ctx, z, group, ctx - group * PEERS


def enter(devices):
    barrier = pltpu.get_barrier_semaphore()
    for device in devices:
        pl.semaphore_signal(barrier, inc=1, device_id=device, device_id_type=MESH)
    pl.semaphore_wait(barrier, len(devices))


def neighbours(ctx, z, group, me):
    peers = [(group * PEERS + wrap(me + d, PEERS), z) for d in range(1, PEERS)]
    right, left = (ctx, wrap(z + 1, RING)), (ctx, wrap(z + RING - 1, RING))
    groups = lax.axis_size("ctx") // PEERS
    above = (wrap(group + 1, groups) * PEERS + me, z)
    below = (wrap(group + groups - 1, groups) * PEERS + me, z)
    return peers, right, left, above, below


def remote(src, dst, send, recv, device):
    return pltpu.make_async_remote_copy(
        src_ref=src, dst_ref=dst, send_sem=send, recv_sem=recv, device_id=device, device_id_type=MESH
    )


def kernel(
    length_ref, q_ref, k_ref, v_ref, g_ref, att_out, dq_out, dk_out, dv_out,
    kv, qs, gs, acc, out, top, total, shift, delta, starts, atts, dqs, sums, mine, buf, halo_buf,
    kv_send, kv_recv, row_send, row_recv, ring_send, ring_recv, halo_send, halo_recv,
    out_send, out_recv, back_send, back_recv, gone_send, gone_recv, last_send, last_recv, own_sem, lengths, length_sem,
):
    ctx, z, group, me = place()
    peers, right, left, above, below = neighbours(ctx, z, group, me)
    base = (group * PEERS - REACH) * SHARD
    fetch = pltpu.make_async_copy(length_ref, lengths, length_sem)
    fetch.start()
    enter(peers + [right, left, above, below])

    def lanes(head, width):
        if isinstance(head, int):
            return pl.ds(head * width, width)
        return pl.ds(pl.multiple_of(head * width, width), width)

    def at(offset):
        return wrap(z + offset, RING)

    def exchange(ref, width, target, send, recv, own):
        copies = [pltpu.make_async_copy(ref.at[:, lanes(me, width)], target, own)]
        for d in range(1, PEERS):
            head = wrap(me + d, PEERS)
            copies.append(
                remote(ref.at[:, lanes(head, width)], target, send.at[d - 1], recv.at[d - 1], peers[d - 1])
            )
        return copies

    chip, core = lax.div(me, 2), lax.rem(me, 2)
    near = (0, 3, 1, 2)

    def key_copy(part, away, other):
        ref = v_ref if part else k_ref
        head = 2 * wrap(chip + away, CHUNKS) + other
        back = (CHUNKS - away) % CHUNKS
        target = kv.at[part, REACH + me, z]
        device = (group * PEERS + head, z)
        sent, come = kv_send.at[part, away, other], kv_recv.at[part, back, core]
        return (
            remote(ref.at[:, lanes(head, D)], target, sent, come, device),
            remote(ref.at[:, lanes(head, D)], target, sent, kv_recv.at[part, away, other], device),
        )

    def cores_of(away):
        return (0, 1) if away else (1 - core,)

    own_keys = [
        pltpu.make_async_copy(ref.at[:, lanes(me, D)], kv.at[part, REACH + me, z], own_sem.at[part])
        for part, ref in enumerate((k_ref, v_ref))
    ]
    query_copies = exchange(q_ref, G * D, qs.at[me], row_send.at[0], row_recv.at[0], own_sem.at[2])
    grad_copies = exchange(g_ref, G * D, gs.at[me], row_send.at[1], row_recv.at[1], own_sem.at[3])
    for copy in own_keys:
        copy.start()
    for away in near:
        for other in cores_of(away):
            for part in range(2):
                key_copy(part, away, other)[0].start()

    positions = (
        base + REACH * SHARD + z * B
        + lax.broadcasted_iota(jnp.int32, (PEERS, B), 0) * SHARD
        + lax.broadcasted_iota(jnp.int32, (PEERS, B), 1)
    )

    fetch.wait()

    def one_doc(number, carried):
        start, vector = carried
        return start + lengths[number], jnp.where(positions >= start, start, vector)

    _, vector = lax.fori_loop(
        0, lengths.shape[0], one_doc, (jnp.int32(0), jnp.zeros((PEERS, B), jnp.int32))
    )
    starts[...] = jnp.concatenate([vector - base] * G, axis=1)
    token = lax.rem(lax.broadcasted_iota(jnp.int32, (1, ROWS), 1), B)

    def chunk_of(turn):
        if isinstance(turn, int):
            return wrap(chip + near[turn], CHUNKS)
        return wrap(chip + 3 * turn + 3 * lax.div(turn, 2) + 2 * lax.div(turn, 3), CHUNKS)

    def ring(way, step, chunk):
        offset = step if way else (RING - step) % RING
        block = kv.at[:, pl.ds(REACH + 2 * chunk, 2), at(offset)]
        return remote(
            block, block, ring_send.at[way, step, chunk], ring_recv.at[way, step, chunk], left if way else right
        )

    def halo(offset):
        return remote(
            kv.at[:, pl.ds(PEERS, REACH), at(offset)], kv.at[:, pl.ds(0, REACH), at(offset)],
            halo_send.at[offset], halo_recv.at[offset], above,
        )

    def arrive(step, turn):
        chunk = chunk_of(turn)
        for way in (0, 1):
            far = (turn >= 2) if way else (turn < 2)
            if step < HOPS:
                ring(way, step - 1, chunk).wait_recv()
            else:
                pl.when(far)(lambda: ring(way, step - 1, chunk).wait_recv())
            if step < HOPS - 1:
                ring(way, step, chunk).start()
            elif step == HOPS - 1:
                pl.when(far)(lambda: ring(way, step, chunk).start())

        @pl.when(chunk == CHUNKS - 1)
        def _():
            halo(step).start()
            if step < HOPS:
                halo(RING - step).start()

    def rows(ref, i):
        return jnp.concatenate([ref[i, :, h * D : (h + 1) * D] for h in range(G)], axis=0)

    def keys_of(i, offset):
        if offset == 0:
            return i, 3
        return i + lax.div(z + offset, RING), 2

    def scores(i, offset, queries):
        slot, count = keys_of(i, offset)
        where = at(offset)
        keys = kv[0, pl.ds(slot, count), where].reshape(count * B, D)
        s = lax.dot_general(keys, queries, (((1,), (1,)), ((), ())), preferred_element_type=F32)
        limit = starts[pl.ds(i, 1), :] - (slot * SHARD + where * B)
        row = lax.broadcasted_iota(jnp.int32, (B, ROWS), 0)
        parts = []
        for n in range(count):
            seen = row >= limit - n * SHARD
            if offset == 0 and n == count - 1:
                seen = seen & (row <= token)
            parts.append(jnp.where(seen, s[n * B : (n + 1) * B], UNSEEN))
        return keys, jnp.concatenate(parts, axis=0)

    def values_of(i, offset):
        slot, count = keys_of(i, offset)
        return kv[1, pl.ds(slot, count), at(offset)].reshape(count * B, D)

    def fold(x, op):
        return op(x.reshape(x.shape[0] // 8, 8, ROWS), axis=0)

    def turned_dot(a, b):
        return lax.dot_general(a, b, (((0,), (0,)), ((), ())), preferred_element_type=F32)

    def forward(pair, offset):
        blocks = (2 * pair, 2 * pair + 1)
        found = [scores(i, offset, rows(qs, i))[1] for i in blocks]
        high = [jnp.max(fold(s, jnp.max), axis=0, keepdims=True) for s in found]
        before = [None if offset == 0 else top[pl.ds(i, 1), :] for i in blocks]
        if offset:
            high = [jnp.maximum(a, b) for a, b in zip(high, before)]
        e = [jnp.exp2((s - h) * (SCALE * LOG2E)) for s, h in zip(found, high)]
        found = [turned_dot(values_of(i, offset), x.astype(BF16)) for i, x in zip(blocks, e)]
        count = [fold(x, jnp.sum) for x in e]
        if offset:
            less = [jnp.exp2((b - h) * (SCALE * LOG2E)) for b, h in zip(before, high)]
            found = [acc[i] * f + o for i, f, o in zip(blocks, less, found)]
            count = [total[i] * f + c for i, f, c in zip(blocks, less, count)]
        for i, h, o, c in zip(blocks, high, found, count):
            top[pl.ds(i, 1), :] = h
            acc[i] = o
            total[i] = c

    def four(step, offsets):
        def turn(k, carried):
            if step is not None:
                arrive(step, k)

            @pl.when(k == CHUNKS - 1)
            def _():
                for offset in offsets:
                    halo(offset).wait_recv()

            pair = lax.rem(k + 1, PEERS // 2)
            for offset in offsets:
                forward(pair, offset)
            return carried

        lax.fori_loop(0, CHUNKS, turn, 0)

    for copy in own_keys:
        copy.wait()
    for turn, away in enumerate(near):
        for other in cores_of(away):
            for part in range(2):
                key_copy(part, away, other)[1].wait_recv()
        chunk = chunk_of(turn)
        for way in (0, 1):
            ring(way, 0, chunk).start()
        pl.when(chunk == CHUNKS - 1)(halo(0).start)
    for copy in query_copies:
        copy.start()
    for k in range(CHUNKS):
        arrive(1, k)
    for copy in query_copies:
        copy.wait()
    for copy in grad_copies:
        copy.start()
    four(2, (0, 7, 1))
    four(3, (6, 2))
    four(4, (5, 3))
    four(None, (4,))
    for copy in grad_copies:
        copy.wait()

    def close(i, carried):
        count = jnp.sum(total[i], axis=0, keepdims=True)
        attended = (acc[i] * (1.0 / count)).astype(BF16).astype(F32)
        shift[pl.ds(i, 1), :] = top[pl.ds(i, 1), :] * (SCALE * LOG2E) + jnp.log(count) * LOG2E
        turned = jnp.concatenate([gs[i, :, h * D : (h + 1) * D].astype(F32).T for h in range(G)], axis=1)
        delta[pl.ds(i, 1), :] = jnp.sum(attended * turned, axis=0, keepdims=True)
        out[i] = attended.astype(BF16)
        acc[i] = jnp.zeros((D, ROWS), F32)
        return carried

    lax.fori_loop(0, PEERS, close, 0)

    def turn_back(i, carried):
        for h in range(G):
            atts[i, :, h * D : (h + 1) * D] = out[i, :, h * B : (h + 1) * B].T
        return carried

    def give(ref, target, width, send, recv, own):
        copies = [pltpu.make_async_copy(ref.at[me], target.at[:, lanes(me, width)], own)]
        for d in range(1, PEERS):
            copies.append(
                remote(
                    ref.at[wrap(me + d, PEERS)], target.at[:, lanes(me, width)],
                    send.at[d - 1], recv.at[d - 1], peers[d - 1],
                )
            )
        for copy in copies:
            copy.start()
        return copies

    def backward(pair, offset):
        blocks = (2 * pair, 2 * pair + 1)
        slot, count = keys_of(blocks[0], offset)
        queries, grads = [rows(qs, i) for i in blocks], [rows(gs, i) for i in blocks]
        found = [scores(i, offset, q) for i, q in zip(blocks, queries)]
        dp = [
            lax.dot_general(
                values_of(i, offset), g, (((1,), (1,)), ((), ())), preferred_element_type=F32
            )
            for i, g in zip(blocks, grads)
        ]
        p = [
            jnp.exp2(s * (SCALE * LOG2E) - shift[pl.ds(i, 1), :]) for i, (_, s) in zip(blocks, found)
        ]
        ds = [(a * (b - delta[pl.ds(i, 1), :])).astype(BF16) for i, a, b in zip(blocks, p, dp)]
        dk = [jnp.dot(d, q, preferred_element_type=F32) for d, q in zip(ds, queries)]
        dv = [jnp.dot(a.astype(BF16), g, preferred_element_type=F32) for a, g in zip(p, grads)]
        dq = [turned_dot(keys, d) for (keys, _), d in zip(found, ds)]
        for part, (a, b) in enumerate((dk, dv)):
            middle = a[B:] + b[: (count - 1) * B]
            value = jnp.concatenate([a[:B], middle, b[(count - 1) * B :]], axis=0)
            sums[part, pl.ds(slot, count + 1)] += value.reshape(count + 1, B, D)
        for i, d in zip(blocks, dq):
            acc[i] += d

    def seal(offset, slot, count):
        for part, scale in enumerate((SCALE, 1.0)):
            mine[offset, part, slot : slot + count] = (sums[part, slot : slot + count] * scale).astype(BF16)

    def all_backward(offset, hooks=(), early=0):
        sums[...] = jnp.zeros_like(sums)

        def one(pair, carried):
            @pl.when(pair == 1)
            def _():
                seal(offset, 0, REACH)
                home(offset).start()

            for number, hook in hooks:
                pl.when(pair == number)(hook)
            backward(pair, offset)
            return carried

        lax.fori_loop(0, PEERS // 2, one, 0)
        seal(offset, REACH + 2 * early, PEERS - 2 * early)

    def home(offset):
        return remote(
            mine.at[offset, :, pl.ds(0, REACH)], halo_buf.at[offset],
            back_send.at[offset], back_recv.at[offset], below,
        )

    def piece(chunk, offset):
        return mine.at[offset, :, pl.ds(REACH + 2 * chunk, 2)]

    def add(target, *others):
        target[...] = sum((ref[...].astype(F32) for ref in others), target[...].astype(F32)).astype(BF16)

    def add_halo(offset):
        home(offset).wait_recv()
        add(piece(CHUNKS - 1, offset), halo_buf.at[offset])

    def most(way, chunk):
        return HOPS if (chunk < 2) == (way == 0) else HOPS - 1

    def message(way, hops, chunk):
        first = hops == most(way, chunk)
        source = piece(chunk, (RING - hops) if way else hops) if first else buf.at[way, hops, chunk]
        return remote(
            source, buf.at[way, hops - 1, chunk],
            gone_send.at[way, hops - 1, chunk], gone_recv.at[way, hops - 1, chunk], left if way else right,
        )

    def post(way, hops, *chunks):
        for chunk in chunks:
            if hops < most(way, chunk):
                message(way, hops + 1, chunk).wait_recv()
                add(buf.at[way, hops, chunk], piece(chunk, (RING - hops) if way else hops))
            message(way, hops, chunk).start()

    def after_4():
        add_halo(4)
        post(1, 4, 3)

    def halo_3():
        add_halo(3)
        post(0, 3, 3)

    def early(chunk):
        def hook():
            seal(5, REACH + 2 * chunk, 2)
            post(1, 3, chunk)

        return hook

    def after_5():
        add_halo(5)
        post(1, 3, 3)

    def after_2():
        add_halo(2)
        post(0, 2, 3)

    def after_6():
        add_halo(6)
        post(1, 2, 2)

    def after_1():
        add_halo(1)
        post(0, 1, 2)

    def later_1():
        post(0, 1, 3)
        post(1, 1, 1)

    def later_7():
        post(0, 1, 0)
        post(1, 1, 2)

    all_backward(4)
    post(0, 4, 0, 1)
    post(1, 4, 2)
    all_backward(3, [(1, after_4)])
    post(0, 3, 2)
    all_backward(5, [(1, halo_3), (2, early(0)), (3, early(1))], 2)
    post(0, 3, 0, 1)
    post(1, 3, 2)
    lax.fori_loop(0, PEERS, turn_back, 0)
    given = give(atts, att_out, G * D, out_send.at[0], out_recv.at[0], own_sem.at[4])
    all_backward(2, [(2, after_5)])
    post(0, 2, 2)
    all_backward(6, [(2, after_2)])
    post(0, 2, 0)
    post(1, 2, 0, 1)
    all_backward(1, [(2, after_6)])
    post(0, 2, 1)
    post(1, 2, 3)
    all_backward(7, [(2, after_1)])
    post(1, 1, 0)
    all_backward(0, [(1, later_1), (3, later_7)])

    def close_query(i, carried):
        for h in range(G):
            dqs[i, :, h * D : (h + 1) * D] = (SCALE * acc[i, :, h * B : (h + 1) * B].T).astype(BF16)
        return carried

    lax.fori_loop(0, PEERS, close_query, 0)
    given += give(dqs, dq_out, G * D, out_send.at[1], out_recv.at[1], own_sem.at[5])
    add_halo(7)
    post(0, 1, 1)
    post(1, 1, 3)
    add_halo(0)

    def last(number, j):
        target = dv_out if number else dk_out
        return remote(
            mine.at[0, number, REACH + j], target.at[:, lanes(me, D)],
            last_send.at[number, j], last_recv.at[number, me], (group * PEERS + j, z),
        )

    for chunk in (0, 2, 1, 3):
        for way in (0, 1):
            message(way, 1, chunk).wait_recv()
        add(piece(chunk, 0), buf.at[0, 0, chunk], buf.at[1, 0, chunk])
        for j in (2 * chunk, 2 * chunk + 1):

            @pl.when(j != me)
            def _():
                last(0, j).start()
                last(1, j).start()

    for number, target in enumerate((dk_out, dv_out)):
        given.append(
            pltpu.make_async_copy(
                mine.at[0, number, REACH + me], target.at[:, lanes(me, D)], own_sem.at[6 + number]
            )
        )
        given[-1].start()
    for copy in given:
        copy.wait()
    for j in range(PEERS):

        @pl.when(j != me)
        def _():
            for number, target in enumerate((dk_out, dv_out)):
                remote(
                    mine.at[0, number, REACH + j], target.at[:, lanes(j, D)],
                    last_send.at[number, j], last_recv.at[number, j], (group * PEERS + j, z),
                ).wait()

    for offset in range(RING):
        halo(offset).wait_send()
        home(offset).wait_send()
    for away in near:
        for other in cores_of(away):
            for part in range(2):
                key_copy(part, away, other)[0].wait_send()
    for way in (0, 1):
        for chunk in range(CHUNKS):
            for step in range(most(way, chunk)):
                ring(way, step, chunk_of(chunk)).wait_send()
                message(way, step + 1, chunk).wait_send()


def shards(queries, keys, values, output_gradient, doc_lengths):
    arguments = (doc_lengths, queries, keys, values, output_gradient)
    anywhere = pl.BlockSpec(memory_space=pltpu.HBM)
    dma = pltpu.SemaphoreType.DMA
    block, message = (B, D), (2, 2, B, D)
    peers, hops = (2, PEERS - 1), (2, HOPS, CHUNKS)
    return pl.pallas_call(
        kernel,
        out_shape=[jax.ShapeDtypeStruct(a.shape, BF16) for a in (queries, queries, keys, values)],
        in_specs=[anywhere] * 5,
        out_specs=[anywhere] * 4,
        scratch_shapes=[
            pltpu.VMEM((2, SLOTS, RING) + block, BF16),
            pltpu.VMEM((PEERS, B, G * D), BF16),
            pltpu.VMEM((PEERS, B, G * D), BF16),
            pltpu.VMEM((PEERS, D, ROWS), F32),
            pltpu.VMEM((PEERS, D, ROWS), BF16),
            pltpu.VMEM((PEERS, ROWS), F32),
            pltpu.VMEM((PEERS, 8, ROWS), F32),
            pltpu.VMEM((PEERS, ROWS), F32),
            pltpu.VMEM((PEERS, ROWS), F32),
            pltpu.VMEM((PEERS, ROWS), jnp.int32),
            pltpu.VMEM((PEERS, B, G * D), BF16),
            pltpu.VMEM((PEERS, B, G * D), BF16),
            pltpu.VMEM((2, SLOTS) + block, F32),
            pltpu.VMEM((RING, 2, SLOTS) + block, BF16),
            pltpu.VMEM((2, HOPS, CHUNKS) + message, BF16),
            pltpu.VMEM((RING,) + message, BF16),
            dma((2, CHUNKS, 2)), dma((2, CHUNKS, 2)), dma(peers), dma(peers), dma(hops), dma(hops),
            dma((RING,)), dma((RING,)),
            dma(peers), dma(peers), dma((RING,)), dma((RING,)), dma(hops), dma(hops), dma((2, PEERS)), dma((2, PEERS)),
            dma((8,)),
            pltpu.SMEM(doc_lengths.shape, jnp.int32),
            dma(()),
        ],
        compiler_params=pltpu.CompilerParams(
            collective_id=0, has_side_effects=True, vmem_limit_bytes=50 * 2**20
        ),
        name="attention",
    )(*(pltpu.with_memory_space_constraint(a, pltpu.HBM) for a in arguments))


def solution(mesh):
    rows = P(("ctx", "head"), None)
    return jax.shard_map(
        shards, mesh=mesh, in_specs=(rows, rows, rows, rows, P()), out_specs=(rows,) * 4, check_vma=False
    )
```

```python
import math

import jax
import jax.numpy as jnp
from jax import lax
from jax.experimental import pallas as pl
from jax.experimental.pallas import tpu as pltpu
from jax.sharding import PartitionSpec as P

MESH = pl.DeviceIdType.MESH
D = 128
G = 4
B = 128
PEERS = 8
RING = 8
REACH = 2
SLOTS = PEERS + REACH
CHUNKS = 4
SHARD = RING * B
ROWS = G * B
HOPS = 4
UNSEEN = -1e30
SCALE = D ** (-0.5)
LOG2E = math.log2(math.e)
BF16 = jnp.bfloat16
F32 = jnp.float32


def wrap(a, n):
    return lax.rem(a, n)


def place():
    ctx = lax.axis_index("ctx")
    z = lax.axis_index("head")
    group = lax.div(ctx, PEERS)
    return ctx, z, group, ctx - group * PEERS


def enter(devices):
    barrier = pltpu.get_barrier_semaphore()
    for device in devices:
        pl.semaphore_signal(barrier, inc=1, device_id=device, device_id_type=MESH)
    pl.semaphore_wait(barrier, len(devices))


def neighbours(ctx, z, group, me):
    peers = [(group * PEERS + wrap(me + d, PEERS), z) for d in range(1, PEERS)]
    right, left = (ctx, wrap(z + 1, RING)), (ctx, wrap(z + RING - 1, RING))
    groups = lax.axis_size("ctx") // PEERS
    above = (wrap(group + 1, groups) * PEERS + me, z)
    below = (wrap(group + groups - 1, groups) * PEERS + me, z)
    return peers, right, left, above, below


def remote(src, dst, send, recv, device):
    return pltpu.make_async_remote_copy(
        src_ref=src, dst_ref=dst, send_sem=send, recv_sem=recv, device_id=device, device_id_type=MESH
    )


def kernel(
    length_ref, q_ref, k_ref, v_ref, g_ref, att_out, dq_out, dk_out, dv_out,
    kv, qs, gs, acc, out, top, total, shift, delta, starts, atts, dqs, sums, mine, buf, halo_buf,
    kv_send, kv_recv, row_send, row_recv, ring_send, ring_recv, halo_send, halo_recv,
    out_send, out_recv, back_send, back_recv, gone_send, gone_recv, last_send, last_recv, own_sem, lengths, length_sem,
):
    ctx, z, group, me = place()
    peers, right, left, above, below = neighbours(ctx, z, group, me)
    base = (group * PEERS - REACH) * SHARD
    fetch = pltpu.make_async_copy(length_ref, lengths, length_sem)
    fetch.start()
    enter(peers + [right, left, above, below])

    def lanes(head, width):
        if isinstance(head, int):
            return pl.ds(head * width, width)
        return pl.ds(pl.multiple_of(head * width, width), width)

    def at(offset):
        return wrap(z + offset, RING)

    def exchange(ref, width, target, send, recv, own):
        copies = [pltpu.make_async_copy(ref.at[:, lanes(me, width)], target, own)]
        for d in range(1, PEERS):
            head = wrap(me + d, PEERS)
            copies.append(
                remote(ref.at[:, lanes(head, width)], target, send.at[d - 1], recv.at[d - 1], peers[d - 1])
            )
        return copies

    chip, core = lax.div(me, 2), lax.rem(me, 2)
    near = (0, 3, 1, 2)

    def key_copy(part, away, other):
        ref = v_ref if part else k_ref
        head = 2 * wrap(chip + away, CHUNKS) + other
        back = (CHUNKS - away) % CHUNKS
        target = kv.at[part, REACH + me, z]
        device = (group * PEERS + head, z)
        sent, come = kv_send.at[part, away, other], kv_recv.at[part, back, core]
        return (
            remote(ref.at[:, lanes(head, D)], target, sent, come, device),
            remote(ref.at[:, lanes(head, D)], target, sent, kv_recv.at[part, away, other], device),
        )

    def cores_of(away):
        return (0, 1) if away else (1 - core,)

    own_keys = [
        pltpu.make_async_copy(ref.at[:, lanes(me, D)], kv.at[part, REACH + me, z], own_sem.at[part])
        for part, ref in enumerate((k_ref, v_ref))
    ]
    query_copies = exchange(q_ref, G * D, qs.at[me], row_send.at[0], row_recv.at[0], own_sem.at[2])
    grad_copies = exchange(g_ref, G * D, gs.at[me], row_send.at[1], row_recv.at[1], own_sem.at[3])
    for copy in own_keys:
        copy.start()
    for away in near:
        for other in cores_of(away):
            for part in range(2):
                key_copy(part, away, other)[0].start()

    positions = (
        base + REACH * SHARD + z * B
        + lax.broadcasted_iota(jnp.int32, (PEERS, B), 0) * SHARD
        + lax.broadcasted_iota(jnp.int32, (PEERS, B), 1)
    )

    fetch.wait()

    def one_doc(number, carried):
        start, vector = carried
        return start + lengths[number], jnp.where(positions >= start, start, vector)

    _, vector = lax.fori_loop(
        0, lengths.shape[0], one_doc, (jnp.int32(0), jnp.zeros((PEERS, B), jnp.int32))
    )
    starts[...] = jnp.concatenate([vector - base] * G, axis=1)
    token = lax.rem(lax.broadcasted_iota(jnp.int32, (1, ROWS), 1), B)

    def chunk_of(turn):
        if isinstance(turn, int):
            return wrap(chip + near[turn], CHUNKS)
        return wrap(chip + 3 * turn + 3 * lax.div(turn, 2) + 2 * lax.div(turn, 3), CHUNKS)

    def ring(way, step, chunk):
        offset = step if way else (RING - step) % RING
        block = kv.at[:, pl.ds(REACH + 2 * chunk, 2), at(offset)]
        return remote(
            block, block, ring_send.at[way, step, chunk], ring_recv.at[way, step, chunk], left if way else right
        )

    def halo(offset):
        return remote(
            kv.at[:, pl.ds(PEERS, REACH), at(offset)], kv.at[:, pl.ds(0, REACH), at(offset)],
            halo_send.at[offset], halo_recv.at[offset], above,
        )

    def arrive(step, turn):
        chunk = chunk_of(turn)
        for way in (0, 1):
            far = (turn >= 2) if way else (turn < 2)
            if step < HOPS or far:
                ring(way, step - 1, chunk).wait_recv()
            if step < HOPS - 1:
                ring(way, step, chunk).start()
            elif step == HOPS - 1:
                pl.when(far)(lambda: ring(way, step, chunk).start())

        @pl.when(chunk == CHUNKS - 1)
        def _():
            halo(step).start()
            if step < HOPS:
                halo(RING - step).start()

    def rows(ref, i):
        return jnp.concatenate([ref[i, :, h * D : (h + 1) * D] for h in range(G)], axis=0)

    def keys_of(i, offset):
        if offset == 0:
            return i, 3
        return i + lax.div(z + offset, RING), 2

    def scores(i, offset, queries):
        slot, count = keys_of(i, offset)
        where = at(offset)
        keys = kv[0, pl.ds(slot, count), where].reshape(count * B, D)
        s = lax.dot_general(keys, queries, (((1,), (1,)), ((), ())), preferred_element_type=F32)
        limit = starts[pl.ds(i, 1), :] - (slot * SHARD + where * B)
        row = lax.broadcasted_iota(jnp.int32, (B, ROWS), 0)
        parts = []
        for n in range(count):
            seen = row >= limit - n * SHARD
            if offset == 0 and n == count - 1:
                seen = seen & (row <= token)
            parts.append(jnp.where(seen, s[n * B : (n + 1) * B], UNSEEN))
        return keys, jnp.concatenate(parts, axis=0)

    def values_of(i, offset):
        slot, count = keys_of(i, offset)
        return kv[1, pl.ds(slot, count), at(offset)].reshape(count * B, D)

    def fold(x, op):
        return op(x.reshape(x.shape[0] // 8, 8, ROWS), axis=0)

    def turned_dot(a, b):
        return lax.dot_general(a, b, (((0,), (0,)), ((), ())), preferred_element_type=F32)

    def forward(pair, offset):
        blocks = (2 * pair, 2 * pair + 1)
        found = [scores(i, offset, rows(qs, i))[1] for i in blocks]
        high = [jnp.max(fold(s, jnp.max), axis=0, keepdims=True) for s in found]
        before = [None if offset == 0 else top[pl.ds(i, 1), :] for i in blocks]
        if offset:
            high = [jnp.maximum(a, b) for a, b in zip(high, before)]
        e = [jnp.exp2((s - h) * (SCALE * LOG2E)) for s, h in zip(found, high)]
        found = [turned_dot(values_of(i, offset), x.astype(BF16)) for i, x in zip(blocks, e)]
        count = [fold(x, jnp.sum) for x in e]
        if offset:
            less = [jnp.exp2((b - h) * (SCALE * LOG2E)) for b, h in zip(before, high)]
            found = [acc[i] * f + o for i, f, o in zip(blocks, less, found)]
            count = [total[i] * f + c for i, f, c in zip(blocks, less, count)]
        for i, h, o, c in zip(blocks, high, found, count):
            top[pl.ds(i, 1), :] = h
            acc[i] = o
            total[i] = c

    def four(step, offsets, hooks=()):
        def turn(k, carried):
            if step is not None and step < HOPS:
                arrive(step, k)
            for number, hook in hooks:
                pl.when(k == number)(hook)

            @pl.when(k == CHUNKS - 1)
            def _():
                for offset in offsets:
                    halo(offset).wait_recv()

            pair = lax.rem(k + 1, PEERS // 2)
            for offset in offsets:
                forward(pair, offset)
            return carried

        lax.fori_loop(0, CHUNKS, turn, 0)

    for copy in own_keys:
        copy.wait()
    for turn, away in enumerate(near):
        for other in cores_of(away):
            for part in range(2):
                key_copy(part, away, other)[1].wait_recv()
        chunk = chunk_of(turn)
        for way in (0, 1):
            ring(way, 0, chunk).start()
        pl.when(chunk == CHUNKS - 1)(halo(0).start)
    for copy in query_copies:
        copy.start()
    for k in range(CHUNKS):
        arrive(1, k)
    for copy in query_copies:
        copy.wait()
    for copy in grad_copies:
        copy.start()
    four(2, (0, 7, 1))

    def turn_grads():
        for copy in grad_copies:
            copy.wait()

        def one(i, carried):
            for h in range(G):
                out[i, :, h * B : (h + 1) * B] = gs[i, :, h * D : (h + 1) * D].T
            return carried

        lax.fori_loop(0, PEERS, one, 0)

    def last_arrivals():
        for k in (0, 2, 1, 3):
            arrive(4, k)

    four(3, (6, 2), [(2, turn_grads)])
    four(4, (5, 3), [(3, last_arrivals)])
    four(None, (4,))

    def close(i, carried):
        count = jnp.sum(total[i], axis=0, keepdims=True)
        attended = (acc[i] * (1.0 / count)).astype(BF16).astype(F32)
        shift[pl.ds(i, 1), :] = top[pl.ds(i, 1), :] * (SCALE * LOG2E) + jnp.log(count) * LOG2E
        delta[pl.ds(i, 1), :] = jnp.sum(attended * out[i].astype(F32), axis=0, keepdims=True)
        out[i] = attended.astype(BF16)
        acc[i] = jnp.zeros((D, ROWS), F32)
        return carried

    lax.fori_loop(0, PEERS, close, 0)

    def turn_back(i, carried):
        for h in range(G):
            atts[i, :, h * D : (h + 1) * D] = out[i, :, h * B : (h + 1) * B].T
        return carried

    def give(ref, target, width, send, recv, own):
        copies = [pltpu.make_async_copy(ref.at[me], target.at[:, lanes(me, width)], own)]
        for d in range(1, PEERS):
            copies.append(
                remote(
                    ref.at[wrap(me + d, PEERS)], target.at[:, lanes(me, width)],
                    send.at[d - 1], recv.at[d - 1], peers[d - 1],
                )
            )
        for copy in copies:
            copy.start()
        return copies

    def backward(pair, offset):
        blocks = (2 * pair, 2 * pair + 1)
        slot, count = keys_of(blocks[0], offset)
        queries, grads = [rows(qs, i) for i in blocks], [rows(gs, i) for i in blocks]
        found = [scores(i, offset, q) for i, q in zip(blocks, queries)]
        dp = [
            lax.dot_general(
                values_of(i, offset), g, (((1,), (1,)), ((), ())), preferred_element_type=F32
            )
            for i, g in zip(blocks, grads)
        ]
        p = [
            jnp.exp2(s * (SCALE * LOG2E) - shift[pl.ds(i, 1), :]) for i, (_, s) in zip(blocks, found)
        ]
        ds = [(a * (b - delta[pl.ds(i, 1), :])).astype(BF16) for i, a, b in zip(blocks, p, dp)]
        dk = [jnp.dot(d, q, preferred_element_type=F32) for d, q in zip(ds, queries)]
        dv = [jnp.dot(a.astype(BF16), g, preferred_element_type=F32) for a, g in zip(p, grads)]
        dq = [turned_dot(keys, d) for (keys, _), d in zip(found, ds)]
        for part, (a, b) in enumerate((dk, dv)):
            middle = a[B:] + b[: (count - 1) * B]
            value = jnp.concatenate([a[:B], middle, b[(count - 1) * B :]], axis=0)
            sums[part, pl.ds(slot, count + 1)] += value.reshape(count + 1, B, D)
        for i, d in zip(blocks, dq):
            acc[i] += d

    def seal(offset, slot, count):
        for part, scale in enumerate((SCALE, 1.0)):
            mine[offset, part, slot : slot + count] = (sums[part, slot : slot + count] * scale).astype(BF16)

    def all_backward(offset, hooks=(), early=0):
        sums[...] = jnp.zeros_like(sums)

        def one(pair, carried):
            @pl.when(pair == 1)
            def _():
                seal(offset, 0, REACH)
                home(offset).start()

            for number, hook in hooks:
                pl.when(pair == number)(hook)
            backward(pair, offset)
            return carried

        lax.fori_loop(0, PEERS // 2, one, 0)
        seal(offset, REACH + 2 * early, PEERS - 2 * early)

    def home(offset):
        return remote(
            mine.at[offset, :, pl.ds(0, REACH)], halo_buf.at[offset],
            back_send.at[offset], back_recv.at[offset], below,
        )

    def piece(chunk, offset):
        return mine.at[offset, :, pl.ds(REACH + 2 * chunk, 2)]

    def add(target, *others):
        target[...] = sum((ref[...].astype(F32) for ref in others), target[...].astype(F32)).astype(BF16)

    def add_halo(offset):
        home(offset).wait_recv()
        add(piece(CHUNKS - 1, offset), halo_buf.at[offset])

    def most(way, chunk):
        return HOPS if (chunk < 2) == (way == 0) else HOPS - 1

    def message(way, hops, chunk):
        first = hops == most(way, chunk)
        source = piece(chunk, (RING - hops) if way else hops) if first else buf.at[way, hops, chunk]
        return remote(
            source, buf.at[way, hops - 1, chunk],
            gone_send.at[way, hops - 1, chunk], gone_recv.at[way, hops - 1, chunk], left if way else right,
        )

    def post(way, hops, *chunks):
        for chunk in chunks:
            if hops < most(way, chunk):
                message(way, hops + 1, chunk).wait_recv()
                add(buf.at[way, hops, chunk], piece(chunk, (RING - hops) if way else hops))
            message(way, hops, chunk).start()

    def after_4():
        add_halo(4)
        post(1, 4, 3)

    def halo_3():
        add_halo(3)
        post(0, 3, 3)

    def early(chunk):
        def hook():
            seal(5, REACH + 2 * chunk, 2)
            post(1, 3, chunk)

        return hook

    def after_5():
        add_halo(5)
        post(1, 3, 3)

    def after_2():
        add_halo(2)
        post(0, 2, 3)

    def after_6():
        add_halo(6)
        post(1, 2, 2)

    def after_1():
        add_halo(1)
        post(0, 1, 2)

    def later_1():
        post(0, 1, 3)
        post(1, 1, 1)

    def later_7():
        post(0, 1, 0)
        post(1, 1, 2)

    all_backward(4)
    post(0, 4, 0, 1)
    post(1, 4, 2)
    all_backward(3, [(1, after_4)])
    post(0, 3, 2)
    all_backward(5, [(1, halo_3), (2, early(0)), (3, early(1))], 2)
    post(0, 3, 0, 1)
    post(1, 3, 2)
    lax.fori_loop(0, PEERS, turn_back, 0)
    given = give(atts, att_out, G * D, out_send.at[0], out_recv.at[0], own_sem.at[4])
    all_backward(2, [(2, after_5)])
    post(0, 2, 2)
    all_backward(6, [(2, after_2)])
    post(0, 2, 0)
    post(1, 2, 0, 1)
    all_backward(1, [(2, after_6)])
    post(0, 2, 1)
    post(1, 2, 3)
    all_backward(7, [(2, after_1)])
    post(1, 1, 0)
    all_backward(0, [(1, later_1), (3, later_7)])

    def close_query(i, carried):
        for h in range(G):
            dqs[i, :, h * D : (h + 1) * D] = (SCALE * acc[i, :, h * B : (h + 1) * B].T).astype(BF16)
        return carried

    lax.fori_loop(0, PEERS, close_query, 0)
    given += give(dqs, dq_out, G * D, out_send.at[1], out_recv.at[1], own_sem.at[5])
    add_halo(7)
    post(0, 1, 1)
    post(1, 1, 3)
    add_halo(0)

    def last(number, j):
        target = dv_out if number else dk_out
        return remote(
            mine.at[0, number, REACH + j], target.at[:, lanes(me, D)],
            last_send.at[number, j], last_recv.at[number, me], (group * PEERS + j, z),
        )

    for chunk in (0, 2, 1, 3):
        for way in (0, 1):
            message(way, 1, chunk).wait_recv()
        add(piece(chunk, 0), buf.at[0, 0, chunk], buf.at[1, 0, chunk])
        for j in (2 * chunk, 2 * chunk + 1):

            @pl.when(j != me)
            def _():
                last(0, j).start()
                last(1, j).start()

    for number, target in enumerate((dk_out, dv_out)):
        given.append(
            pltpu.make_async_copy(
                mine.at[0, number, REACH + me], target.at[:, lanes(me, D)], own_sem.at[6 + number]
            )
        )
        given[-1].start()
    for copy in given:
        copy.wait()
    for j in range(PEERS):

        @pl.when(j != me)
        def _():
            for number, target in enumerate((dk_out, dv_out)):
                remote(
                    mine.at[0, number, REACH + j], target.at[:, lanes(j, D)],
                    last_send.at[number, j], last_recv.at[number, j], (group * PEERS + j, z),
                ).wait()

    for offset in range(RING):
        halo(offset).wait_send()
        home(offset).wait_send()
    for away in near:
        for other in cores_of(away):
            for part in range(2):
                key_copy(part, away, other)[0].wait_send()
    for way in (0, 1):
        for chunk in range(CHUNKS):
            for step in range(most(way, chunk)):
                ring(way, step, chunk_of(chunk)).wait_send()
                message(way, step + 1, chunk).wait_send()


def shards(queries, keys, values, output_gradient, doc_lengths):
    arguments = (doc_lengths, queries, keys, values, output_gradient)
    anywhere = pl.BlockSpec(memory_space=pltpu.HBM)
    dma = pltpu.SemaphoreType.DMA
    block, message = (B, D), (2, 2, B, D)
    peers, hops = (2, PEERS - 1), (2, HOPS, CHUNKS)
    return pl.pallas_call(
        kernel,
        out_shape=[jax.ShapeDtypeStruct(a.shape, BF16) for a in (queries, queries, keys, values)],
        in_specs=[anywhere] * 5,
        out_specs=[anywhere] * 4,
        scratch_shapes=[
            pltpu.VMEM((2, SLOTS, RING) + block, BF16),
            pltpu.VMEM((PEERS, B, G * D), BF16),
            pltpu.VMEM((PEERS, B, G * D), BF16),
            pltpu.VMEM((PEERS, D, ROWS), F32),
            pltpu.VMEM((PEERS, D, ROWS), BF16),
            pltpu.VMEM((PEERS, ROWS), F32),
            pltpu.VMEM((PEERS, 8, ROWS), F32),
            pltpu.VMEM((PEERS, ROWS), F32),
            pltpu.VMEM((PEERS, ROWS), F32),
            pltpu.VMEM((PEERS, ROWS), jnp.int32),
            pltpu.VMEM((PEERS, B, G * D), BF16),
            pltpu.VMEM((PEERS, B, G * D), BF16),
            pltpu.VMEM((2, SLOTS) + block, F32),
            pltpu.VMEM((RING, 2, SLOTS) + block, BF16),
            pltpu.VMEM((2, HOPS, CHUNKS) + message, BF16),
            pltpu.VMEM((RING,) + message, BF16),
            dma((2, CHUNKS, 2)), dma((2, CHUNKS, 2)), dma(peers), dma(peers), dma(hops), dma(hops),
            dma((RING,)), dma((RING,)),
            dma(peers), dma(peers), dma((RING,)), dma((RING,)), dma(hops), dma(hops), dma((2, PEERS)), dma((2, PEERS)),
            dma((8,)),
            pltpu.SMEM(doc_lengths.shape, jnp.int32),
            dma(()),
        ],
        compiler_params=pltpu.CompilerParams(
            collective_id=0, has_side_effects=True, vmem_limit_bytes=50 * 2**20
        ),
        name="attention",
    )(*(pltpu.with_memory_space_constraint(a, pltpu.HBM) for a in arguments))


def solution(mesh):
    rows = P(("ctx", "head"), None)
    return jax.shard_map(
        shards, mesh=mesh, in_specs=(rows, rows, rows, rows, P()), out_specs=(rows,) * 4, check_vma=False
    )
```
